32 devices in a mesh: rep: 2 (over x), node: 2 (over core), ep: 8 (over z, y).
Axes of the slice: x: 2, y: 2, z: 4, core: 2. Of those that a mesh axis runs over, the one named last changes fastest.
Arguments:
- activations: bfloat16 [3072, 7168], P(('rep', 'node', 'ep')), parts along dimension 0, may hold values from -6 to 6
- expert_ids: int32 [3072, 8], P(('rep', 'node', 'ep')), parts along dimension 0, may hold values from 0 to 255, all different within a row; in each aligned block of 96 rows (0 to 95, 96 to 191, ...) at most 8 rows name the same one
- route_scores: float32 [3072, 8], P(('rep', 'node', 'ep')), parts along dimension 0, may hold values from 0.05 to 1
- capacity: int32 [256], replicated, may hold values from 6 to 8
- w_gate: bfloat16 [7168, 4096], P(None, ('node', 'ep')), may hold values from -0.0625 to 0.0625
- w_up: bfloat16 [7168, 4096], P(None, ('node', 'ep')), may hold values from -0.0625 to 0.0625
- w_down: bfloat16 [4096, 7168], P(('node', 'ep')), may hold values from -0.125 to 0.125
Outputs:
- mixed_out: bfloat16 [3072, 7168], P(('rep', 'node', 'ep')), parts along dimension 0
The draws below stay inside these ranges and needn't reach their ends.
There are 2 independent parts, one for each index of `rep`. The reference program is written for one: setup_inputs(seed, part) draws one part's arguments, and reference() takes and returns one part's arrays. A program takes and returns all parts, laid end to end along the dimension named above; an argument that names none is the same for every part. Nothing has to cross between parts.
Inputs may be any that keep to these rules, and one draw needn't show every extreme that they name: `expert_ids`: each row names 8 different experts. In each aligned block of 96 rows (the rows of one device) no expert is named by more than 8 rows, and in some block one expert is named by exactly 8 rows.
All inputs are finite; a program needn't handle non-finite values.
Results may differ from the reference program's by a relative error of at most 0.007.
Values may be sent and summed in bfloat16 or wider, within the bound.
A program may use at most 128 MiB of HBM per device.

```python
import math
import jax
import jax.numpy as jnp
import numpy as np
from jax import lax

D = 7168
FF = 2048
EXPERTS = 256
TOPK = 8
SHARDS = 8
TOK_DEV = 96
HID_DEV = 256
SEND_CAP = 8
CAP_LO = 6
EXP_WIN = 2
TOKENS = 1536
N_NODE = 2
N_EP = 8


def draw_capacity(key, part):
    key_values, key_order = jax.random.split(jax.random.fold_in(key, 11))
    limits = jax.random.randint(key_values, (EXPERTS,), CAP_LO, SEND_CAP + 1)
    chosen = jax.random.permutation(key_order, EXPERTS)
    limits = limits.at[chosen[0]].set(CAP_LO)
    limits = limits.at[chosen[1]].set(SEND_CAP)
    return limits.astype(jnp.int32)


def level_of(key, dims, shards, low, top_value):
    gain, own = 1.0, jax.random.fold_in(key, 6)
    for position, shards_of in shards:
        draws = jnp.exp(jax.random.uniform(jax.random.fold_in(own, position), (shards_of,), jnp.float32, low / len(shards), top_value / len(shards)))
        gain = gain * jnp.repeat(draws, dims[position] // shards_of).reshape([-1 if axis == position else 1 for axis in range(len(dims))])
    return gain


def assign_block(stream_key, own, number, rows, number_of, top, limit, skew):
    order = jax.random.permutation(stream_key, number_of)
    heavy_load, usual = load_shares(number_of, rows * top, limit, skew, True), load_shares(number_of, rows * top, limit, skew, False)
    places = jnp.arange(number_of)

    def named(sizes, offset_by):
        used = int((sizes > 0).sum())
        fixed = max(1, used // 4)
        moved = fixed + (places - fixed + offset_by * (used - fixed)) % max(1, number_of - fixed)
        return jnp.zeros((number_of,), jnp.int32).at[order[jnp.where(places < fixed, places, moved)]].set(jnp.asarray(sizes, jnp.int32))

    sizes = jnp.where(number % 4 == 0, named(heavy_load, number // 4), named(usual, number - number // 4 - 1))
    mixed = jax.random.permutation(jax.random.fold_in(own, 3), number_of)
    donor, receiver = mixed[0:number_of // 2 * 2:2], mixed[1:number_of // 2 * 2:2]
    slack = jnp.minimum(sizes[donor] - 1, limit - sizes[receiver]) // 2
    slack = jnp.where((donor == order[0]) | (receiver == order[0]) | (sizes[receiver] == 0), 0, jnp.maximum(slack, 0))
    moved = jax.random.randint(jax.random.fold_in(own, 4), (number_of // 2,), 0, 1 << 20) % (slack + 1)
    sizes = sizes.at[donor].add(-moved).at[receiver].add(moved)
    members = jnp.searchsorted(jnp.cumsum(sizes), jnp.arange(rows * top), side="right").astype(jnp.int32)
    table = members.reshape(top, rows).T
    table = table[jax.random.permutation(jax.random.fold_in(own, 1), rows)]
    offset_by = jax.random.randint(jax.random.fold_in(own, 2), (rows, 1), 0, top)
    return jnp.take_along_axis(table, (jnp.arange(top)[None, :] + offset_by) % top, axis=1)


def load_shares(number_of, total, most, lean, full):
    loads = [(1 << 20) // math.isqrt(standing ** lean) + 1 for standing in range(1, number_of + 1)]
    largest = most if full else min(most, max(-(-total // number_of), total * loads[0] // sum(loads)))
    least = 1 if total - largest >= number_of - 1 else 0
    holding, spare = [largest] + [least] * (number_of - 1), total - largest - least * (number_of - 1)
    while spare > 0:
        free = [i for i in range(1, number_of) if holding[i] < largest] or [i for i in range(1, number_of) if holding[i] < most]
        pool, remaining = sum([loads[i] for i in free]), spare
        for i in free:
            more = min(most - holding[i], max(1, remaining * loads[i] // pool), spare)
            holding[i] = holding[i] + more
            spare = spare - more
    return np.array(holding)


def centred(stream_key, shape, deviation, reach, shards=(), kind=jnp.bfloat16):
    drawn = jax.random.normal(stream_key, shape, jnp.float32) * deviation
    if len(shards) > 0:
        drawn = level_of(stream_key, shape, shards, -0.22, 0.18) * drawn
    return jnp.clip(drawn, min=-reach, max=reach).astype(kind)


def setup_inputs(seed: int = 0, part: int = 0) -> dict:
    splits = jax.random.split(jax.random.key(seed), 8)
    part_keys = jax.random.split(jax.random.fold_in(splits[7], part), 8)
    activations = centred(part_keys[0], (TOKENS, D), 1.0, 6.0, ((0, 16),))
    expert_ids_keys = jax.random.split(jax.random.fold_in(part_keys[1], 1), TOKENS // TOK_DEV)
    expert_ids_turns = jax.random.permutation(jax.random.fold_in(part_keys[1], 3), TOKENS // TOK_DEV)
    expert_ids = jax.vmap(lambda own, number: assign_block(jax.random.fold_in(part_keys[1], 2), own, number, TOK_DEV, EXPERTS, TOPK, SEND_CAP, 2))(expert_ids_keys, expert_ids_turns).reshape((TOKENS, TOPK))
    route_scores = jnp.clip(jnp.exp(math.log(1.0) - 2.9957323 * jax.random.uniform(part_keys[2], (TOKENS, TOPK), jnp.float32) ** level_of(part_keys[2], (TOKENS, TOPK), ((0, 16),), -0.2, 0.2)), 0.05, 1.0)
    capacity = draw_capacity(jax.random.fold_in(splits[7], 71), part)
    w_gate = centred(splits[4], (D, EXP_WIN * FF), D ** -0.5, 0.0625, ((1, 16),))
    w_up = centred(splits[5], (D, EXP_WIN * FF), D ** -0.5, 0.0625, ((1, 16),))
    w_down = centred(splits[6], (EXP_WIN * FF, D), FF ** -0.5, 0.125, ((0, 16),))
    return dict(activations=activations, expert_ids=expert_ids, route_scores=route_scores, capacity=capacity, w_gate=w_gate, w_up=w_up, w_down=w_down)


def reference(activations, expert_ids, route_scores, capacity, w_gate, w_up, w_down):
    blocks = N_NODE * N_EP
    window = EXP_WIN
    route_weight = (2.5 * route_scores / jnp.sum(route_scores, axis=1, keepdims=True)).astype(jnp.bfloat16)
    flat_ids = expert_ids.reshape(blocks, TOK_DEV * TOPK)
    expert_iota = jnp.arange(window, dtype=jnp.int32)
    onehot = (flat_ids[:, :, None] == expert_iota[None, None, :]).astype(jnp.int32)
    running = jnp.cumsum(onehot, axis=1)
    ranking = jnp.sum(onehot * running, axis=2) - 1
    limits = jnp.sum(onehot * capacity[:window][None, None, :], axis=2)
    is_live = (flat_ids < window) & (ranking < limits)
    block_id = jnp.arange(blocks, dtype=jnp.int32)[:, None]
    token_id = block_id * TOK_DEV + jnp.arange(TOK_DEV * TOPK, dtype=jnp.int32)[None, :] // TOPK
    table_size = blocks * SEND_CAP * window
    target = jnp.where(is_live, (block_id * SEND_CAP + ranking) * window + flat_ids, table_size).astype(jnp.int32)
    slot_table = jnp.full((table_size,), TOKENS, jnp.int32)
    slot_table = slot_table.at[target.reshape(-1)].set(token_id.reshape(-1).astype(jnp.int32), mode="drop")
    padded = jnp.concatenate([activations, jnp.zeros((1, D), activations.dtype)], axis=0)
    row_block = padded[slot_table].reshape(blocks * SEND_CAP, window, D)
    outputs = []
    for expert in range(window):
        expert_rows = row_block[:, expert]
        gate_act = jnp.dot(expert_rows, w_gate[:, expert * FF:(expert + 1) * FF], preferred_element_type=jnp.float32)
        up_act = jnp.dot(expert_rows, w_up[:, expert * FF:(expert + 1) * FF], preferred_element_type=jnp.float32)
        inner_act = (jax.nn.silu(gate_act) * up_act).astype(jnp.bfloat16)
        total_out = jnp.zeros((blocks * SEND_CAP, D), jnp.float32)
        for shard_idx in range(SHARDS):
            start = expert * FF + shard_idx * HID_DEV
            piece_out = jnp.dot(inner_act[:, shard_idx * HID_DEV:(shard_idx + 1) * HID_DEV], w_down[start:start + HID_DEV], preferred_element_type=jnp.float32).astype(jnp.bfloat16)
            total_out = total_out + lax.optimization_barrier(piece_out).astype(jnp.float32)
        outputs.append(total_out.astype(jnp.bfloat16))
    expert_out = jnp.stack(outputs, axis=1).reshape(table_size, D)
    live_tok = is_live.reshape(TOKENS, TOPK)
    target_tok = target.reshape(TOKENS, TOPK)
    mixed_out = jnp.zeros((TOKENS, D), jnp.float32)
    for entry in range(TOPK):
        picked = expert_out[jnp.minimum(target_tok[:, entry], table_size - 1)].astype(jnp.float32)
        weight_k = jnp.where(live_tok[:, entry], route_weight[:, entry].astype(jnp.float32), 0.0)
        mixed_out = mixed_out + weight_k[:, None] * picked
    return mixed_out.astype(jnp.bfloat16)
```

```python
import functools

import jax
import jax.numpy as jnp
from jax import lax
from jax.experimental import pallas as pl
from jax.experimental.pallas import tpu as pltpu
from jax.sharding import PartitionSpec as P

MESH = pl.DeviceIdType.MESH
TOPK = 8
SHARDS = 8
SEND_CAP = 8
SIDE = 2
PIECES = 2


def shards(activations, expert_ids, route_scores, capacity, w_gate, w_up, w_down):
    n_node = lax.axis_size("node")
    n_ep = lax.axis_size("ep")
    window = n_node * (n_ep // SHARDS)
    tok_rows = activations.shape[0]
    model_width = activations.shape[1]
    send_cap = SEND_CAP
    route_weight = (2.5 * route_scores / jnp.sum(route_scores, axis=1, keepdims=True)).astype(
        jnp.bfloat16
    )
    flat_ids = expert_ids.reshape(-1)
    expert_iota = jnp.arange(window, dtype=jnp.int32)
    onehot = (flat_ids[:, None] == expert_iota[None, :]).astype(jnp.int32)
    running = jnp.cumsum(onehot, axis=0)
    ranking = jnp.sum(onehot * running, axis=1) - 1
    limits = jnp.sum(onehot * capacity[:window][None, :], axis=1)
    is_live = (flat_ids < window) & (ranking < limits)
    slot_index = jnp.where(is_live, ranking * window + flat_ids, -1).reshape(tok_rows, TOPK)
    positions = jnp.arange(send_cap * window, dtype=jnp.int32)
    matches = slot_index[:, :, None] == positions[None, None, :]
    select = jnp.any(matches, axis=1).astype(jnp.bfloat16)
    combine_w = jnp.sum(
        jnp.where(matches, route_weight[:, :, None].astype(jnp.float32), 0.0), axis=1
    ).astype(jnp.bfloat16)
    expert_rows = lax.dot_general(
        select, activations, (((0,), (0,)), ((), ())), preferred_element_type=jnp.float32
    ).astype(jnp.bfloat16)
    copies = jnp.broadcast_to(
        expert_rows.reshape(send_cap, window, 1, model_width),
        (send_cap, window, SHARDS, model_width),
    )
    copies = copies.reshape(send_cap, window * SHARDS * model_width)
    received = lax.all_to_all(copies, ("node", "ep"), split_axis=1, concat_axis=0, tiled=True)
    gate_act = jnp.dot(received, w_gate, preferred_element_type=jnp.float32)
    up_act = jnp.dot(received, w_up, preferred_element_type=jnp.float32)
    inner_act = (jax.nn.silu(gate_act) * up_act).astype(jnp.bfloat16)
    partial_value = jnp.dot(inner_act, w_down, preferred_element_type=jnp.float32).astype(
        jnp.bfloat16
    )
    returned = lax.all_to_all(
        partial_value, ("node", "ep"), split_axis=0, concat_axis=1, tiled=True
    )
    summed = jnp.sum(
        returned.reshape(send_cap, window, SHARDS, model_width).astype(jnp.float32), axis=2
    )
    expert_out = summed.astype(jnp.bfloat16).reshape(send_cap * window, model_width)
    mixed_out = jnp.dot(combine_w, expert_out, preferred_element_type=jnp.float32)
    return mixed_out.astype(jnp.bfloat16)


def chunk_of(width):
    for size in (1024, 512, 256):
        if width % size == 0:
            return size
    return 128


def expert_kernel(
    line, a_ref, wg_hbm, wu_hbm, wd_hbm, out_ref,
    wg, wu, wd, gate_sum, up_sum, xb, core_in, part, side_in, up_in, down_in, stage,
    w_sem, core_sem, up_sem, down_sem, side_sem, zrecv_sem, yrecv_sem,
    p_side_sem, p_side_recv, p_up_sem, p_up_recv, p_down_sem, p_down_recv, last_sem, last_recv,
):
    node = lax.axis_index("node")
    ep = lax.axis_index("ep")
    z, y = ep // SIDE, ep % SIDE
    other = 1 - y
    rows, width = a_ref.shape[1], a_ref.shape[2]
    piece = width // PIECES
    to_core = {"node": 1 - node}
    to_side = {"ep": z * SIDE + other}
    to_up = {"ep": ep + SIDE}
    to_down = {"ep": ep - SIDE}
    has_up, has_down = z < line - 1, z > 0

    loads = [
        pltpu.make_async_copy(src, dst, w_sem.at[i])
        for i, (src, dst) in enumerate(((wg_hbm, wg), (wu_hbm, wu), (wd_hbm, wd)))
    ]
    for load in loads:
        load.start()

    barrier = pltpu.get_barrier_semaphore()
    pl.semaphore_signal(barrier, inc=1, device_id=to_core, device_id_type=MESH)
    pl.semaphore_signal(barrier, inc=1, device_id=to_side, device_id_type=MESH)

    @pl.when(has_up)
    def _():
        pl.semaphore_signal(barrier, inc=1, device_id=to_up, device_id_type=MESH)

    @pl.when(has_down)
    def _():
        pl.semaphore_signal(barrier, inc=1, device_id=to_down, device_id_type=MESH)

    pl.semaphore_wait(barrier, 2 + has_up.astype(jnp.int32) + has_down.astype(jnp.int32))

    def cols(c):
        return pl.ds(c * piece, piece)

    def remote(src, dst, send, recv, where):
        return pltpu.make_async_remote_copy(
            src_ref=src, dst_ref=dst, send_sem=send, recv_sem=recv,
            device_id=where, device_id_type=MESH,
        )

    def core_copy(c):
        return remote(
            a_ref.at[1 - node, :, cols(c)], core_in.at[:, cols(c)],
            core_sem.at[0, c], core_sem.at[1, c], to_core,
        )

    def x_copy(o, c, send, recv, where):
        ref = xb.at[o * SIDE + y, :, cols(c)]
        return remote(ref, ref, send.at[o, c], recv.at[o, c], where)

    def x_up(o, c):
        return x_copy(o, c, up_sem, zrecv_sem, to_up)

    def x_down(o, c):
        return x_copy(o, c, down_sem, zrecv_sem, to_down)

    def x_side(o, c):
        return x_copy(o, c, side_sem, yrecv_sem, to_side)

    for c in range(PIECES):
        core_copy(c).start()
    for c in range(PIECES):
        core_copy(c).wait_recv()
        xb[ep, :, cols(c)] = a_ref[node, :, cols(c)] + core_in[:, cols(c)]
        pl.when(has_up)(lambda c=c: x_up(z, c).start())
        pl.when(has_down)(lambda c=c: x_down(z, c).start())
        x_side(z, c).start()

    for d in range(1, line):
        for c in range(PIECES):
            @pl.when(z - d >= 0)
            def _():
                x_up(z - d, c).wait_recv()
                pl.when(has_up)(lambda: x_up(z - d, c).start())
                x_side(z - d, c).start()

            @pl.when(z + d < line)
            def _():
                x_down(z + d, c).wait_recv()
                pl.when(has_down)(lambda: x_down(z + d, c).start())
                x_side(z + d, c).start()

    for o in range(line):
        for c in range(PIECES):
            x_side(o, c).wait_recv()

    count = xb.shape[0] * rows
    loads[0].wait()
    loads[1].wait()
    gate_sum[...] = jnp.zeros_like(gate_sum)
    up_sum[...] = jnp.zeros_like(up_sum)
    step = chunk_of(width)

    @pl.loop(0, width // step)
    def _(k):
        at = pl.ds(pl.multiple_of(k * step, step), step)
        x = xb[:, :, at].reshape(count, step)
        gate_sum[...] += jnp.dot(x, wg[at, :], preferred_element_type=jnp.float32)
        up_sum[...] += jnp.dot(x, wu[at, :], preferred_element_type=jnp.float32)

    gate = gate_sum[...]
    inner = (gate / (1.0 + jnp.exp(-gate)) * up_sum[...]).astype(jnp.bfloat16)
    loads[2].wait()
    step = chunk_of(piece)

    def p_side(t, c):
        return remote(
            part.at[t * SIDE + other, :, cols(c)], side_in.at[t, :, cols(c)],
            p_side_sem.at[t, c], p_side_recv.at[t, c], to_side,
        )

    def p_up(t, c):
        return remote(
            stage.at[t, :, cols(c)], up_in.at[t, :, cols(c)],
            p_up_sem.at[t, c], p_up_recv.at[t, c], to_up,
        )

    def p_down(t, c):
        return remote(
            stage.at[t, :, cols(c)], down_in.at[t, :, cols(c)],
            p_down_sem.at[t, c], p_down_recv.at[t, c], to_down,
        )

    def last(c):
        ref = out_ref.at[node, :, cols(c)]
        return remote(ref, ref, last_sem.at[c], last_recv.at[c], to_core)

    for c in range(PIECES):
        @pl.loop(0, piece // step)
        def _(k):
            at = pl.ds(pl.multiple_of(c * piece + k * step, step), step)
            value = jnp.dot(inner, wd[:, at], preferred_element_type=jnp.float32)
            part[:, :, at] = value.astype(part.dtype).reshape(part.shape[0], rows, step)

        for d in range(line - 1, 0, -1):
            pl.when(z + d < line)(lambda: p_side(z + d, c).start())
            pl.when(z - d >= 0)(lambda: p_side(z - d, c).start())
        p_side(z, c).start()

    def f32(ref, t, c):
        return ref[t, :, cols(c)].astype(jnp.float32)

    def here(t, c):
        return f32(part, t * SIDE + y, c) + f32(side_in, t, c)

    for c in range(PIECES):
        for d in range(line - 1, 0, -1):
            @pl.when(z + d < line)
            def _():
                t = z + d
                p_side(t, c).wait_recv()

                @pl.when(has_down)
                def _():
                    p_up(t, c).wait_recv()
                    stage[t, :, cols(c)] = (here(t, c) + f32(up_in, t, c)).astype(stage.dtype)

                @pl.when(z == 0)
                def _():
                    stage[t, :, cols(c)] = here(t, c).astype(stage.dtype)

                p_up(t, c).start()

            @pl.when(z - d >= 0)
            def _():
                t = z - d
                p_side(t, c).wait_recv()

                @pl.when(has_up)
                def _():
                    p_down(t, c).wait_recv()
                    stage[t, :, cols(c)] = (here(t, c) + f32(down_in, t, c)).astype(stage.dtype)

                @pl.when(z == line - 1)
                def _():
                    stage[t, :, cols(c)] = here(t, c).astype(stage.dtype)

                p_down(t, c).start()

        p_side(z, c).wait_recv()

        @pl.when(has_down)
        def _():
            p_up(z, c).wait_recv()

        @pl.when(has_up)
        def _():
            p_down(z, c).wait_recv()

        @pl.when(has_down & has_up)
        def _():
            total = here(z, c) + f32(up_in, z, c) + f32(down_in, z, c)
            out_ref[node, :, cols(c)] = total.astype(out_ref.dtype)

        @pl.when(z == 0)
        def _():
            total = here(z, c) + f32(down_in, z, c)
            out_ref[node, :, cols(c)] = total.astype(out_ref.dtype)

        @pl.when(z == line - 1)
        def _():
            total = here(z, c) + f32(up_in, z, c)
            out_ref[node, :, cols(c)] = total.astype(out_ref.dtype)

        last(c).start()

    for c in range(PIECES):
        core_copy(c).wait_send()
        x_side(z, c).wait_send()
        pl.when(has_up)(lambda: x_up(z, c).wait_send())
        pl.when(has_down)(lambda: x_down(z, c).wait_send())
        p_side(z, c).wait_send()
        for d in range(1, line):
            @pl.when(z - d >= 0)
            def _():
                pl.when(has_up)(lambda: x_up(z - d, c).wait_send())
                x_side(z - d, c).wait_send()
                p_side(z - d, c).wait_send()
                p_down(z - d, c).wait_send()

            @pl.when(z + d < line)
            def _():
                pl.when(has_down)(lambda: x_down(z + d, c).wait_send())
                x_side(z + d, c).wait_send()
                p_side(z + d, c).wait_send()
                p_up(z + d, c).wait_send()

        last(c).wait_recv()
        last(c).wait_send()


def run_experts(rows_by_expert, w_gate, w_up, w_down):
    experts, rows, width = rows_by_expert.shape
    n_ep = lax.axis_size("ep")
    line = n_ep // SIDE
    hidden = w_gate.shape[1]
    kind = rows_by_expert.dtype
    count = n_ep * rows
    vmem = pltpu.VMEM
    sems = pltpu.SemaphoreType.DMA
    flops = 6 * count * width * hidden
    return pl.pallas_call(
        functools.partial(expert_kernel, line),
        out_shape=jax.ShapeDtypeStruct((experts, rows, width), kind),
        in_specs=[pl.BlockSpec(memory_space=pltpu.VMEM)] + [pl.BlockSpec(memory_space=pl.ANY)] * 3,
        out_specs=pl.BlockSpec(memory_space=pltpu.VMEM),
        scratch_shapes=[
            vmem(w_gate.shape, kind),
            vmem(w_up.shape, kind),
            vmem(w_down.shape, kind),
            vmem((count, hidden), jnp.float32),
            vmem((count, hidden), jnp.float32),
            vmem((n_ep, rows, width), kind),
            vmem((rows, width), kind),
            vmem((n_ep, rows, width), kind),
            vmem((line, rows, width), kind),
            vmem((line, rows, width), kind),
            vmem((line, rows, width), kind),
            vmem((line, rows, width), kind),
            sems((3,)),
            sems((2, PIECES)),
        ]
        + [sems((line, PIECES))] * 11
        + [sems((PIECES,))] * 2,
        compiler_params=pltpu.CompilerParams(
            collective_id=0, has_side_effects=True, vmem_limit_bytes=48 * 1024 * 1024
        ),
        cost_estimate=pl.CostEstimate(
            flops=flops, bytes_accessed=6 * width * hidden, transcendentals=count * hidden
        ),
        name="routed_experts",
    )(rows_by_expert, w_gate, w_up, w_down)


def grid_shards(activations, expert_ids, route_scores, capacity, w_gate, w_up, w_down):
    cores = lax.axis_size("node")
    tok_rows, width = activations.shape
    window = cores
    route_weight = (2.5 * route_scores / jnp.sum(route_scores, axis=1, keepdims=True)).astype(
        jnp.bfloat16
    )
    flat_ids = expert_ids.reshape(-1)
    expert_iota = jnp.arange(window, dtype=jnp.int32)
    onehot = (flat_ids[:, None] == expert_iota[None, :]).astype(jnp.int32)
    running = jnp.cumsum(onehot, axis=0)
    ranking = jnp.sum(onehot * running, axis=1) - 1
    limits = jnp.sum(onehot * capacity[:window][None, :], axis=1)
    is_live = (flat_ids < window) & (ranking < limits)
    mine = lax.axis_index("node") * SEND_CAP
    slots = cores * SEND_CAP
    slot_index = jnp.where(is_live, flat_ids * slots + mine + ranking, -1).reshape(tok_rows, TOPK)
    positions = jnp.arange(window * slots, dtype=jnp.int32)
    matches = slot_index[:, :, None] == positions[None, None, :]
    select = jnp.any(matches, axis=1).astype(jnp.bfloat16)
    combine_w = jnp.sum(
        jnp.where(matches, route_weight[:, :, None].astype(jnp.float32), 0.0), axis=1
    ).astype(jnp.bfloat16)
    sent = lax.dot_general(
        select, activations, (((0,), (0,)), ((), ())), preferred_element_type=jnp.float32
    ).astype(jnp.bfloat16)
    expert_out = run_experts(sent.reshape(window, slots, width), w_gate, w_up, w_down)
    mixed_out = jnp.dot(
        combine_w, expert_out.reshape(window * slots, width), preferred_element_type=jnp.float32
    )
    return mixed_out.astype(jnp.bfloat16)


def solution(mesh):
    placed = (
        P(("rep", "node", "ep"), None),
        P(("rep", "node", "ep"), None),
        P(("rep", "node", "ep"), None),
        P(),
        P(None, ("node", "ep")),
        P(None, ("node", "ep")),
        P(("node", "ep"), None),
    )
    fits = mesh.shape["ep"] == SHARDS and mesh.shape["node"] == 2
    return jax.shard_map(
        grid_shards if fits else shards,
        mesh=mesh,
        in_specs=placed,
        out_specs=P(("rep", "node", "ep"), None),
        check_vma=False,
    )
```

```python
import functools

import jax
import jax.numpy as jnp
from jax import lax
from jax.experimental import pallas as pl
from jax.experimental.pallas import tpu as pltpu
from jax.sharding import PartitionSpec as P

MESH = pl.DeviceIdType.MESH
TOPK = 8
SHARDS = 8
SEND_CAP = 8
SIDE = 2


def shards(activations, expert_ids, route_scores, capacity, w_gate, w_up, w_down):
    n_node = lax.axis_size("node")
    n_ep = lax.axis_size("ep")
    window = n_node * (n_ep // SHARDS)
    tok_rows = activations.shape[0]
    model_width = activations.shape[1]
    send_cap = SEND_CAP
    route_weight = (2.5 * route_scores / jnp.sum(route_scores, axis=1, keepdims=True)).astype(
        jnp.bfloat16
    )
    flat_ids = expert_ids.reshape(-1)
    expert_iota = jnp.arange(window, dtype=jnp.int32)
    onehot = (flat_ids[:, None] == expert_iota[None, :]).astype(jnp.int32)
    running = jnp.cumsum(onehot, axis=0)
    ranking = jnp.sum(onehot * running, axis=1) - 1
    limits = jnp.sum(onehot * capacity[:window][None, :], axis=1)
    is_live = (flat_ids < window) & (ranking < limits)
    slot_index = jnp.where(is_live, ranking * window + flat_ids, -1).reshape(tok_rows, TOPK)
    positions = jnp.arange(send_cap * window, dtype=jnp.int32)
    matches = slot_index[:, :, None] == positions[None, None, :]
    select = jnp.any(matches, axis=1).astype(jnp.bfloat16)
    combine_w = jnp.sum(
        jnp.where(matches, route_weight[:, :, None].astype(jnp.float32), 0.0), axis=1
    ).astype(jnp.bfloat16)
    expert_rows = lax.dot_general(
        select, activations, (((0,), (0,)), ((), ())), preferred_element_type=jnp.float32
    ).astype(jnp.bfloat16)
    copies = jnp.broadcast_to(
        expert_rows.reshape(send_cap, window, 1, model_width),
        (send_cap, window, SHARDS, model_width),
    )
    copies = copies.reshape(send_cap, window * SHARDS * model_width)
    received = lax.all_to_all(copies, ("node", "ep"), split_axis=1, concat_axis=0, tiled=True)
    gate_act = jnp.dot(received, w_gate, preferred_element_type=jnp.float32)
    up_act = jnp.dot(received, w_up, preferred_element_type=jnp.float32)
    inner_act = (jax.nn.silu(gate_act) * up_act).astype(jnp.bfloat16)
    partial_value = jnp.dot(inner_act, w_down, preferred_element_type=jnp.float32).astype(
        jnp.bfloat16
    )
    returned = lax.all_to_all(
        partial_value, ("node", "ep"), split_axis=0, concat_axis=1, tiled=True
    )
    summed = jnp.sum(
        returned.reshape(send_cap, window, SHARDS, model_width).astype(jnp.float32), axis=2
    )
    expert_out = summed.astype(jnp.bfloat16).reshape(send_cap * window, model_width)
    mixed_out = jnp.dot(combine_w, expert_out, preferred_element_type=jnp.float32)
    return mixed_out.astype(jnp.bfloat16)


def piece_of(width):
    for size in (1024, 512, 256):
        if width % size == 0:
            return size
    return 128


def select_rows(node, experts, ids_ref, score_ref, cap_ref):
    ids, scores = ids_ref[...], score_ref[...]
    tokens = ids.shape[0]
    slots = experts * SEND_CAP
    weight = (2.5 * scores / jnp.sum(scores, axis=1, keepdims=True)).astype(jnp.bfloat16)
    weight = weight.astype(jnp.float32)
    column = lax.broadcasted_iota(jnp.int32, (tokens, experts * slots), 1)
    rank_of = column % slots - node * SEND_CAP
    hit = jnp.zeros(column.shape, jnp.float32)
    hit_weight = jnp.zeros(column.shape, jnp.float32)
    limit = jnp.zeros(column.shape, jnp.int32)
    for e in range(experts):
        named = ids == e
        here = column // slots == e
        any_named = jnp.sum(jnp.where(named, 1.0, 0.0), axis=1, keepdims=True)
        its_weight = jnp.sum(jnp.where(named, weight, 0.0), axis=1, keepdims=True)
        hit = jnp.where(here, any_named, hit)
        hit_weight = jnp.where(here, its_weight, hit_weight)
        limit = jnp.where(here, cap_ref[e], limit)
    before = lax.broadcasted_iota(jnp.int32, (tokens, tokens), 0) > lax.broadcasted_iota(
        jnp.int32, (tokens, tokens), 1
    )
    rank = jnp.dot(
        jnp.where(before, 1.0, 0.0).astype(jnp.bfloat16),
        hit.astype(jnp.bfloat16),
        preferred_element_type=jnp.float32,
    ).astype(jnp.int32)
    live = (hit > 0.5) & (rank == rank_of) & (rank_of >= 0) & (rank_of < SEND_CAP) & (rank < limit)
    select = jnp.where(live, 1.0, 0.0).astype(jnp.bfloat16)
    return select, jnp.where(live, hit_weight, 0.0).astype(jnp.bfloat16)


def expert_kernel(
    line, cap_ref, ids_ref, score_ref, act_ref, wg_hbm, wu_hbm, wd_hbm, out_ref, mix_ref,
    wg, wu, wd, gate_sum, up_sum, sent, xb, core_in, part,
    side_in, up_in, down_in, stage, far_up, far_down, far_stage,
    w_sem, core_sem, up_sem, down_sem, side_sem, zrecv_sem, yrecv_sem,
    p_side_sem, p_side_recv, p_up_sem, p_up_recv, p_down_sem, p_down_recv, last_sem, last_recv,
    far_sem,
):
    node = lax.axis_index("node")
    ep = lax.axis_index("ep")
    z, y = ep // SIDE, ep % SIDE
    other = 1 - y
    experts, rows, width = sent.shape
    piece = far_stage.shape[2]
    pieces = width // piece
    to_core = {"node": 1 - node}
    to_side = {"ep": z * SIDE + other}
    to_up = {"ep": ep + SIDE}
    to_down = {"ep": ep - SIDE}
    has_up, has_down = z < line - 1, z > 0

    loads = [
        pltpu.make_async_copy(src, dst, w_sem.at[i])
        for i, (src, dst) in enumerate(((wg_hbm, wg), (wu_hbm, wu), (wd_hbm, wd)))
    ]
    for load in loads:
        load.start()

    barrier = pltpu.get_barrier_semaphore()
    pl.semaphore_signal(barrier, inc=1, device_id=to_core, device_id_type=MESH)
    pl.semaphore_signal(barrier, inc=1, device_id=to_side, device_id_type=MESH)

    @pl.when(has_up)
    def _():
        pl.semaphore_signal(barrier, inc=1, device_id=to_up, device_id_type=MESH)

    @pl.when(has_down)
    def _():
        pl.semaphore_signal(barrier, inc=1, device_id=to_down, device_id_type=MESH)

    def cols(c):
        return pl.ds(c * piece, piece)

    def remote(src, dst, send, recv, where):
        return pltpu.make_async_remote_copy(
            src_ref=src, dst_ref=dst, send_sem=send, recv_sem=recv,
            device_id=where, device_id_type=MESH,
        )

    def core_copy(c):
        return remote(
            sent.at[1 - node, :, cols(c)], core_in.at[:, cols(c)],
            core_sem.at[0, c], core_sem.at[1, c], to_core,
        )

    def x_copy(o, c, send, recv, where):
        ref = xb.at[o * SIDE + y, :, cols(c)]
        return remote(ref, ref, send.at[o, c], recv.at[o, c], where)

    def x_up(o, c):
        return x_copy(o, c, up_sem, zrecv_sem, to_up)

    def x_down(o, c):
        return x_copy(o, c, down_sem, zrecv_sem, to_down)

    def x_side(o, c):
        return x_copy(o, c, side_sem, yrecv_sem, to_side)

    def far(o, i, where):
        ref = xb.at[o * SIDE + other, :, cols(0)]
        return remote(ref, ref, far_sem.at[i, o], far_sem.at[2, o], where)

    def x_far_up(o):
        return far(o, 0, to_up)

    def x_far_down(o):
        return far(o, 1, to_down)

    select, mix = select_rows(node, experts, ids_ref, score_ref, cap_ref)
    mix_ref[...] = mix
    for c in range(pieces):
        taken = lax.dot_general(
            select, act_ref[:, cols(c)], (((0,), (0,)), ((), ())),
            preferred_element_type=jnp.float32,
        )
        sent[:, :, cols(c)] = taken.astype(sent.dtype).reshape(experts, rows, piece)
        if c == 0:
            pl.semaphore_wait(barrier, 2 + has_up.astype(jnp.int32) + has_down.astype(jnp.int32))
        core_copy(c).start()
    for c in range(pieces):
        core_copy(c).wait_recv()
        xb[ep, :, cols(c)] = sent[node, :, cols(c)] + core_in[:, cols(c)]
        x_side(z, c).start()
        pl.when(has_up)(lambda: x_up(z, c).start())
        pl.when(has_down)(lambda: x_down(z, c).start())

    x_side(z, 0).wait_recv()
    pl.when(has_up)(lambda: x_far_up(z).start())
    pl.when(has_down)(lambda: x_far_down(z).start())

    for d in range(1, line):
        for c in range(pieces):
            @pl.when(z - d >= 0)
            def _():
                x_up(z - d, c).wait_recv()
                pl.when(has_up)(lambda: x_up(z - d, c).start())
                if c > 0:
                    x_side(z - d, c).start()

            @pl.when(z + d < line)
            def _():
                x_down(z + d, c).wait_recv()
                pl.when(has_down)(lambda: x_down(z + d, c).start())
                if c > 0:
                    x_side(z + d, c).start()

        @pl.when(z - d >= 0)
        def _():
            x_far_up(z - d).wait_recv()
            pl.when(has_up)(lambda: x_far_up(z - d).start())

        @pl.when(z + d < line)
        def _():
            x_far_down(z + d).wait_recv()
            pl.when(has_down)(lambda: x_far_down(z + d).start())

    count = xb.shape[0] * rows
    loads[0].wait()
    loads[1].wait()
    for c in range(pieces):
        if c > 0:
            for o in range(line):
                x_side(o, c).wait_recv()
        x = xb[:, :, cols(c)].reshape(count, piece)
        gate_part = jnp.dot(x, wg[cols(c), :], preferred_element_type=jnp.float32)
        up_part = jnp.dot(x, wu[cols(c), :], preferred_element_type=jnp.float32)
        if c == 0:
            gate_sum[...] = gate_part
            up_sum[...] = up_part
        else:
            gate_sum[...] += gate_part
            up_sum[...] += up_part

    gate = gate_sum[...]
    inner = (gate / (1.0 + jnp.exp(-gate)) * up_sum[...]).astype(jnp.bfloat16)
    loads[2].wait()

    def p_side(t, c):
        src = far_stage.at[t] if c == 0 else part.at[t * SIDE + other, :, cols(c)]
        return remote(
            src, side_in.at[t, :, cols(c)],
            p_side_sem.at[t, c], p_side_recv.at[t, c], to_side,
        )

    def p_up(t, c):
        return remote(
            stage.at[t, :, cols(c)], up_in.at[t, :, cols(c)],
            p_up_sem.at[t, c], p_up_recv.at[t, c], to_up,
        )

    def p_down(t, c):
        return remote(
            stage.at[t, :, cols(c)], down_in.at[t, :, cols(c)],
            p_down_sem.at[t, c], p_down_recv.at[t, c], to_down,
        )

    def p_far_up(t):
        return remote(far_stage.at[t], far_up.at[t], far_sem.at[3, t], far_sem.at[4, t], to_up)

    def p_far_down(t):
        return remote(far_stage.at[t], far_down.at[t], far_sem.at[5, t], far_sem.at[6, t], to_down)

    def last(c):
        ref = out_ref.at[node, :, cols(c)]
        return remote(ref, ref, last_sem.at[c], last_recv.at[c], to_core)

    def at_distance(d, act):
        pl.when(z + d < line)(lambda: act(z + d, True))
        pl.when(z - d >= 0)(lambda: act(z - d, False))

    def f32(ref, t, c):
        return ref[t, :, cols(c)].astype(jnp.float32)

    def here(t, c):
        own = f32(part, t * SIDE + y, c)
        return own if c == 0 else own + f32(side_in, t, c)

    def there(t):
        return f32(part, t * SIDE + other, 0)

    def pass_on(t, c, upward):
        if c > 0:
            p_side(t, c).wait_recv()
        copy, arrived = (p_up, up_in) if upward else (p_down, down_in)
        more, end = (has_down, z == 0) if upward else (has_up, z == line - 1)

        @pl.when(more)
        def _():
            copy(t, c).wait_recv()
            stage[t, :, cols(c)] = (here(t, c) + f32(arrived, t, c)).astype(stage.dtype)

        @pl.when(end)
        def _():
            stage[t, :, cols(c)] = here(t, c).astype(stage.dtype)

        copy(t, c).start()

    def pass_far(t, upward):
        copy, arrived = (p_far_up, far_up) if upward else (p_far_down, far_down)
        more, end = (has_down, z == 0) if upward else (has_up, z == line - 1)

        @pl.when(more)
        def _():
            copy(t).wait_recv()
            far_stage[t] = (there(t) + arrived[t].astype(jnp.float32)).astype(far_stage.dtype)

        @pl.when(end)
        def _():
            far_stage[t] = there(t).astype(far_stage.dtype)

        copy(t).start()

    order = list(range(1, pieces)) + [0]
    for c in order:
        value = jnp.dot(inner, wd[:, cols(c)], preferred_element_type=jnp.float32)
        part[:, :, cols(c)] = value.astype(part.dtype).reshape(part.shape[0], rows, piece)
        if c > 0:
            at_distance(line - 1, lambda t, upward: p_side(t, c).start())
            if line > 2:
                at_distance(line - 2, lambda t, upward: p_side(t, c).start())
    for d in range(line - 3, 0, -1):
        for c in range(1, pieces):
            at_distance(d, lambda t, upward: p_side(t, c).start())
    for c in range(1, pieces):
        p_side(z, c).start()

    for d in range(line - 1, 0, -1):
        at_distance(d, lambda t, upward: pass_on(t, 0, upward))
        at_distance(d, pass_far)
        for c in range(1, pieces):
            at_distance(d, lambda t, upward: pass_on(t, c, upward))

    def far_sum(with_up, with_down):
        total = there(z)
        if with_up:
            total = total + far_up[z].astype(jnp.float32)
        if with_down:
            total = total + far_down[z].astype(jnp.float32)
        far_stage[z] = total.astype(far_stage.dtype)

    def near_sum(c, with_up, with_down):
        total = f32(part, ep, c) + f32(side_in, z, c)
        if with_up:
            total = total + f32(up_in, z, c)
        if with_down:
            total = total + f32(down_in, z, c)
        out_ref[node, :, cols(c)] = total.astype(out_ref.dtype)

    def by_place(add):
        pl.when(has_down & has_up)(lambda: add(True, True))
        pl.when(z == 0)(lambda: add(False, True))
        pl.when(z == line - 1)(lambda: add(True, False))

    pl.when(has_down)(lambda: p_far_up(z).wait_recv())
    pl.when(has_up)(lambda: p_far_down(z).wait_recv())
    by_place(far_sum)
    p_side(z, 0).start()
    for c in order:
        p_side(z, c).wait_recv()
        pl.when(has_down)(lambda: p_up(z, c).wait_recv())
        pl.when(has_up)(lambda: p_down(z, c).wait_recv())
        by_place(lambda with_up, with_down: near_sum(c, with_up, with_down))
        last(c).start()

    def done_far(t, upward):
        pl.when(has_down if upward else has_up)(
            lambda: (x_far_down if upward else x_far_up)(t).wait_send()
        )
        (p_far_up if upward else p_far_down)(t).wait_send()

    def done(t, c, upward):
        pl.when(has_down if upward else has_up)(
            lambda: (x_down if upward else x_up)(t, c).wait_send()
        )
        if c > 0:
            x_side(t, c).wait_send()
            p_side(t, c).wait_send()
        (p_up if upward else p_down)(t, c).wait_send()

    pl.when(has_up)(lambda: x_far_up(z).wait_send())
    pl.when(has_down)(lambda: x_far_down(z).wait_send())
    for d in range(1, line):
        at_distance(d, done_far)
    for c in range(pieces):
        core_copy(c).wait_send()
        x_side(z, c).wait_send()
        pl.when(has_up)(lambda: x_up(z, c).wait_send())
        pl.when(has_down)(lambda: x_down(z, c).wait_send())
        p_side(z, c).wait_send()
        for d in range(1, line):
            at_distance(d, lambda t, upward: done(t, c, upward))
    for c in order:
        last(c).wait_recv()
        last(c).wait_send()


def run_experts(activations, expert_ids, route_scores, capacity, w_gate, w_up, w_down):
    experts = lax.axis_size("node")
    n_ep = lax.axis_size("ep")
    tokens, width = activations.shape
    rows = experts * SEND_CAP
    line = n_ep // SIDE
    hidden = w_gate.shape[1]
    kind = activations.dtype
    count = n_ep * rows
    piece = piece_of(width)
    pieces = width // piece
    vmem = pltpu.VMEM
    sems = pltpu.SemaphoreType.DMA
    here = pl.BlockSpec(memory_space=pltpu.VMEM)
    return pl.pallas_call(
        functools.partial(expert_kernel, line),
        out_shape=(
            jax.ShapeDtypeStruct((experts, rows, width), kind),
            jax.ShapeDtypeStruct((tokens, experts * rows), jnp.bfloat16),
        ),
        in_specs=[pl.BlockSpec(memory_space=pltpu.SMEM)]
        + [here] * 3
        + [pl.BlockSpec(memory_space=pl.ANY)] * 3,
        out_specs=(here, here),
        scratch_shapes=[
            vmem(w_gate.shape, kind),
            vmem(w_up.shape, kind),
            vmem(w_down.shape, kind),
            vmem((count, hidden), jnp.float32),
            vmem((count, hidden), jnp.float32),
            vmem((experts, rows, width), kind),
            vmem((n_ep, rows, width), kind),
            vmem((rows, width), kind),
            vmem((n_ep, rows, width), kind),
        ]
        + [vmem((line, rows, width), kind)] * 4
        + [vmem((line, rows, piece), kind)] * 3
        + [sems((3,)), sems((2, pieces))]
        + [sems((line, pieces))] * 11
        + [sems((pieces,))] * 2
        + [sems((7, line))],
        compiler_params=pltpu.CompilerParams(
            collective_id=0, has_side_effects=True, vmem_limit_bytes=48 * 1024 * 1024
        ),
        cost_estimate=pl.CostEstimate(
            flops=6 * count * width * hidden,
            bytes_accessed=6 * width * hidden,
            transcendentals=count * hidden,
        ),
        name="routed_experts",
    )(capacity, expert_ids, route_scores, activations, w_gate, w_up, w_down)


def grid_shards(activations, expert_ids, route_scores, capacity, w_gate, w_up, w_down):
    expert_out, combine_w = run_experts(
        activations, expert_ids, route_scores, capacity, w_gate, w_up, w_down
    )
    mixed_out = jnp.dot(
        combine_w,
        expert_out.reshape(-1, expert_out.shape[2]),
        preferred_element_type=jnp.float32,
    )
    return mixed_out.astype(jnp.bfloat16)


def solution(mesh):
    placed = (
        P(("rep", "node", "ep"), None),
        P(("rep", "node", "ep"), None),
        P(("rep", "node", "ep"), None),
        P(),
        P(None, ("node", "ep")),
        P(None, ("node", "ep")),
        P(("node", "ep"), None),
    )
    fits = mesh.shape["ep"] == SHARDS and mesh.shape["node"] == 2
    return jax.shard_map(
        grid_shards if fits else shards,
        mesh=mesh,
        in_specs=placed,
        out_specs=P(("rep", "node", "ep"), None),
        check_vma=False,
    )
```

```python
import functools

import jax
import jax.numpy as jnp
from jax import lax
from jax.experimental import pallas as pl
from jax.experimental.pallas import tpu as pltpu
from jax.sharding import PartitionSpec as P

MESH = pl.DeviceIdType.MESH
TOPK = 8
SHARDS = 8
SEND_CAP = 8
SIDE = 2


def shards(activations, expert_ids, route_scores, capacity, w_gate, w_up, w_down):
    n_node = lax.axis_size("node")
    n_ep = lax.axis_size("ep")
    window = n_node * (n_ep // SHARDS)
    tok_rows = activations.shape[0]
    model_width = activations.shape[1]
    send_cap = SEND_CAP
    route_weight = (2.5 * route_scores / jnp.sum(route_scores, axis=1, keepdims=True)).astype(
        jnp.bfloat16
    )
    flat_ids = expert_ids.reshape(-1)
    expert_iota = jnp.arange(window, dtype=jnp.int32)
    onehot = (flat_ids[:, None] == expert_iota[None, :]).astype(jnp.int32)
    running = jnp.cumsum(onehot, axis=0)
    ranking = jnp.sum(onehot * running, axis=1) - 1
    limits = jnp.sum(onehot * capacity[:window][None, :], axis=1)
    is_live = (flat_ids < window) & (ranking < limits)
    slot_index = jnp.where(is_live, ranking * window + flat_ids, -1).reshape(tok_rows, TOPK)
    positions = jnp.arange(send_cap * window, dtype=jnp.int32)
    matches = slot_index[:, :, None] == positions[None, None, :]
    select = jnp.any(matches, axis=1).astype(jnp.bfloat16)
    combine_w = jnp.sum(
        jnp.where(matches, route_weight[:, :, None].astype(jnp.float32), 0.0), axis=1
    ).astype(jnp.bfloat16)
    expert_rows = lax.dot_general(
        select, activations, (((0,), (0,)), ((), ())), preferred_element_type=jnp.float32
    ).astype(jnp.bfloat16)
    copies = jnp.broadcast_to(
        expert_rows.reshape(send_cap, window, 1, model_width),
        (send_cap, window, SHARDS, model_width),
    )
    copies = copies.reshape(send_cap, window * SHARDS * model_width)
    received = lax.all_to_all(copies, ("node", "ep"), split_axis=1, concat_axis=0, tiled=True)
    gate_act = jnp.dot(received, w_gate, preferred_element_type=jnp.float32)
    up_act = jnp.dot(received, w_up, preferred_element_type=jnp.float32)
    inner_act = (jax.nn.silu(gate_act) * up_act).astype(jnp.bfloat16)
    partial_value = jnp.dot(inner_act, w_down, preferred_element_type=jnp.float32).astype(
        jnp.bfloat16
    )
    returned = lax.all_to_all(
        partial_value, ("node", "ep"), split_axis=0, concat_axis=1, tiled=True
    )
    summed = jnp.sum(
        returned.reshape(send_cap, window, SHARDS, model_width).astype(jnp.float32), axis=2
    )
    expert_out = summed.astype(jnp.bfloat16).reshape(send_cap * window, model_width)
    mixed_out = jnp.dot(combine_w, expert_out, preferred_element_type=jnp.float32)
    return mixed_out.astype(jnp.bfloat16)


def piece_of(width):
    for size in (1024, 512, 256):
        if width % size == 0:
            return size
    return 128


def select_rows(node, experts, ids_ref, score_ref, cap_ref):
    ids, scores = ids_ref[...], score_ref[...]
    tokens = ids.shape[1]
    slots = experts * SEND_CAP
    weight = (2.5 * scores / jnp.sum(scores, axis=0, keepdims=True)).astype(jnp.bfloat16)
    weight = weight.astype(jnp.float32)
    line = lax.broadcasted_iota(jnp.int32, (experts * slots, tokens), 0)
    rank_of = line % slots - node * SEND_CAP
    hit = jnp.zeros(line.shape, jnp.float32)
    hit_weight = jnp.zeros(line.shape, jnp.float32)
    limit = jnp.zeros(line.shape, jnp.int32)
    for e in range(experts):
        named = ids == e
        here = line // slots == e
        any_named = jnp.sum(jnp.where(named, 1.0, 0.0), axis=0, keepdims=True)
        its_weight = jnp.sum(jnp.where(named, weight, 0.0), axis=0, keepdims=True)
        hit = jnp.where(here, any_named, hit)
        hit_weight = jnp.where(here, its_weight, hit_weight)
        limit = jnp.where(here, cap_ref[e], limit)
    before = lax.broadcasted_iota(jnp.int32, (tokens, tokens), 0) < lax.broadcasted_iota(
        jnp.int32, (tokens, tokens), 1
    )
    rank = jnp.dot(
        hit.astype(jnp.bfloat16),
        jnp.where(before, 1.0, 0.0).astype(jnp.bfloat16),
        preferred_element_type=jnp.float32,
    ).astype(jnp.int32)
    live = (hit > 0.5) & (rank == rank_of) & (rank_of >= 0) & (rank_of < SEND_CAP) & (rank < limit)
    select = jnp.where(live, 1.0, 0.0).astype(jnp.bfloat16)
    return select, jnp.where(live, hit_weight, 0.0).astype(jnp.bfloat16)


def expert_kernel(
    line, cap_ref, ids_ref, score_ref, act_hbm, wg_hbm, wu_hbm, wd_hbm, out_ref, mix_ref,
    act, wg, wu, wd, gate_sum, up_sum, sent, xb, core_in, part,
    side_in, up_in, down_in, stage, far_up, far_down, far_stage,
    w_sem, core_sem, up_sem, down_sem, side_sem, zrecv_sem, yrecv_sem,
    p_side_sem, p_side_recv, p_up_sem, p_up_recv, p_down_sem, p_down_recv, last_sem, last_recv,
    far_sem, end_sem,
):
    node = lax.axis_index("node")
    ep = lax.axis_index("ep")
    z, y = ep // SIDE, ep % SIDE
    other = 1 - y
    experts, rows, width = sent.shape
    piece = far_stage.shape[2]
    pieces = width // piece
    to_core = {"node": 1 - node}
    to_side = {"ep": z * SIDE + other}
    to_up = {"ep": ep + SIDE}
    to_down = {"ep": ep - SIDE}
    to_end = {"ep": (line - 1 - z) * SIDE + y}
    has_up, has_down = z < line - 1, z > 0
    at_end = (z == 0) | (z == line - 1)

    loads = [
        pltpu.make_async_copy(src, dst, w_sem.at[i])
        for i, (src, dst) in enumerate(((act_hbm, act), (wg_hbm, wg), (wu_hbm, wu), (wd_hbm, wd)))
    ]
    for load in loads:
        load.start()

    barrier = pltpu.get_barrier_semaphore()
    pl.semaphore_signal(barrier, inc=1, device_id=to_core, device_id_type=MESH)
    pl.semaphore_signal(barrier, inc=1, device_id=to_side, device_id_type=MESH)

    @pl.when(has_up)
    def _():
        pl.semaphore_signal(barrier, inc=1, device_id=to_up, device_id_type=MESH)

    @pl.when(has_down)
    def _():
        pl.semaphore_signal(barrier, inc=1, device_id=to_down, device_id_type=MESH)

    @pl.when(at_end)
    def _():
        pl.semaphore_signal(barrier, inc=1, device_id=to_end, device_id_type=MESH)

    def cols(c):
        return pl.ds(c * piece, piece)

    def remote(src, dst, send, recv, where):
        return pltpu.make_async_remote_copy(
            src_ref=src, dst_ref=dst, send_sem=send, recv_sem=recv,
            device_id=where, device_id_type=MESH,
        )

    def core_copy(c):
        return remote(
            sent.at[1 - node, :, cols(c)], core_in.at[:, cols(c)],
            core_sem.at[0, c], core_sem.at[1, c], to_core,
        )

    def x_copy(o, c, send, recv, where):
        ref = xb.at[o * SIDE + y, :, cols(c)]
        return remote(ref, ref, send.at[o, c], recv.at[o, c], where)

    def x_up(o, c):
        return x_copy(o, c, up_sem, zrecv_sem, to_up)

    def x_down(o, c):
        return x_copy(o, c, down_sem, zrecv_sem, to_down)

    def x_side(o, c):
        return x_copy(o, c, side_sem, yrecv_sem, to_side)

    def far(o, i, where):
        ref = xb.at[o * SIDE + other, :, cols(0)]
        return remote(ref, ref, far_sem.at[i, o], far_sem.at[2, o], where)

    def x_far_up(o):
        return far(o, 0, to_up)

    def x_far_down(o):
        return far(o, 1, to_down)

    def x_end(c):
        ref = xb.at[ep, :, cols(c)]
        return remote(ref, ref, end_sem.at[c], zrecv_sem.at[z, c], to_end)

    def x_far_end():
        ref = xb.at[z * SIDE + other, :, cols(0)]
        return remote(ref, ref, end_sem.at[pieces], far_sem.at[2, z], to_end)

    select, mix = select_rows(node, experts, ids_ref, score_ref, cap_ref)
    mix_ref[...] = mix
    loads[0].wait()
    for c in range(pieces):
        taken = jnp.dot(select, act[:, cols(c)], preferred_element_type=jnp.float32)
        sent[:, :, cols(c)] = taken.astype(sent.dtype).reshape(experts, rows, piece)
        if c == 0:
            pl.semaphore_wait(barrier, 4)
        core_copy(c).start()
    for c in range(pieces):
        core_copy(c).wait_recv()
        xb[ep, :, cols(c)] = sent[node, :, cols(c)] + core_in[:, cols(c)]
        x_side(z, c).start()
        pl.when(has_up)(lambda: x_up(z, c).start())
        pl.when(has_down)(lambda: x_down(z, c).start())

    x_side(z, 0).wait_recv()
    pl.when(has_up)(lambda: x_far_up(z).start())
    pl.when(has_down)(lambda: x_far_down(z).start())

    @pl.when(at_end)
    def _():
        for c in range(pieces):
            x_end(c).start()
        x_far_end().start()

    def relay(d, more):
        return pl.when(more) if d < line - 2 else (lambda act: None)

    for d in range(1, line):
        for c in range(pieces):
            @pl.when(z - d >= 0)
            def _():
                x_up(z - d, c).wait_recv()
                relay(d, has_up)(lambda: x_up(z - d, c).start())
                if c > 0:
                    x_side(z - d, c).start()

            @pl.when(z + d < line)
            def _():
                x_down(z + d, c).wait_recv()
                relay(d, has_down)(lambda: x_down(z + d, c).start())
                if c > 0:
                    x_side(z + d, c).start()

        @pl.when(z - d >= 0)
        def _():
            x_far_up(z - d).wait_recv()
            relay(d, has_up)(lambda: x_far_up(z - d).start())

        @pl.when(z + d < line)
        def _():
            x_far_down(z + d).wait_recv()
            relay(d, has_down)(lambda: x_far_down(z + d).start())

    count = xb.shape[0] * rows
    loads[1].wait()
    loads[2].wait()
    for c in range(pieces):
        if c > 0:
            for o in range(line):
                x_side(o, c).wait_recv()
        x = xb[:, :, cols(c)].reshape(count, piece)
        gate_part = jnp.dot(x, wg[cols(c), :], preferred_element_type=jnp.float32)
        up_part = jnp.dot(x, wu[cols(c), :], preferred_element_type=jnp.float32)
        if c == 0:
            gate_sum[...] = gate_part
            up_sum[...] = up_part
        else:
            gate_sum[...] += gate_part
            up_sum[...] += up_part

    gate = gate_sum[...]
    inner = (gate / (1.0 + jnp.exp(-gate)) * up_sum[...]).astype(jnp.bfloat16)
    loads[3].wait()

    def p_side(t, c):
        src = far_stage.at[t] if c == 0 else part.at[t * SIDE + other, :, cols(c)]
        return remote(
            src, side_in.at[t, :, cols(c)],
            p_side_sem.at[t, c], p_side_recv.at[t, c], to_side,
        )

    def p_up(t, c):
        return remote(
            stage.at[t, :, cols(c)], up_in.at[t, :, cols(c)],
            p_up_sem.at[t, c], p_up_recv.at[t, c], to_up,
        )

    def p_down(t, c):
        return remote(
            stage.at[t, :, cols(c)], down_in.at[t, :, cols(c)],
            p_down_sem.at[t, c], p_down_recv.at[t, c], to_down,
        )

    def p_far_up(t):
        return remote(far_stage.at[t], far_up.at[t], far_sem.at[3, t], far_sem.at[4, t], to_up)

    def p_far_down(t):
        return remote(far_stage.at[t], far_down.at[t], far_sem.at[5, t], far_sem.at[6, t], to_down)

    def last(c):
        ref = out_ref.at[node, :, cols(c)]
        return remote(ref, ref, last_sem.at[c], last_recv.at[c], to_core)

    def at_distance(d, act):
        pl.when(z + d < line)(lambda: act(z + d, True))
        pl.when(z - d >= 0)(lambda: act(z - d, False))

    def f32(ref, t, c):
        return ref[t, :, cols(c)].astype(jnp.float32)

    def here(t, c):
        own = f32(part, t * SIDE + y, c)
        return own if c == 0 else own + f32(side_in, t, c)

    def there(t):
        return f32(part, t * SIDE + other, 0)

    def pass_on(t, c, upward):
        if c > 0:
            p_side(t, c).wait_recv()
        copy, arrived = (p_up, up_in) if upward else (p_down, down_in)
        more, end = (has_down, z == 0) if upward else (has_up, z == line - 1)

        @pl.when(more)
        def _():
            copy(t, c).wait_recv()
            stage[t, :, cols(c)] = (here(t, c) + f32(arrived, t, c)).astype(stage.dtype)

        @pl.when(end)
        def _():
            stage[t, :, cols(c)] = here(t, c).astype(stage.dtype)

        copy(t, c).start()

    def pass_far(t, upward):
        copy, arrived = (p_far_up, far_up) if upward else (p_far_down, far_down)
        more, end = (has_down, z == 0) if upward else (has_up, z == line - 1)

        @pl.when(more)
        def _():
            copy(t).wait_recv()
            far_stage[t] = (there(t) + arrived[t].astype(jnp.float32)).astype(far_stage.dtype)

        @pl.when(end)
        def _():
            far_stage[t] = there(t).astype(far_stage.dtype)

        copy(t).start()

    order = list(range(1, pieces)) + [0]
    for c in order:
        value = jnp.dot(inner, wd[:, cols(c)], preferred_element_type=jnp.float32)
        part[:, :, cols(c)] = value.astype(part.dtype).reshape(part.shape[0], rows, piece)
        if c > 0:
            at_distance(line - 1, lambda t, upward: p_side(t, c).start())
            if line > 2:
                at_distance(line - 2, lambda t, upward: p_side(t, c).start())
    for d in range(line - 3, 0, -1):
        for c in range(1, pieces):
            at_distance(d, lambda t, upward: p_side(t, c).start())
    for c in range(1, pieces):
        p_side(z, c).start()

    for d in range(line - 1, 0, -1):
        at_distance(d, lambda t, upward: pass_on(t, 0, upward))
        at_distance(d, pass_far)
        for c in range(1, pieces):
            at_distance(d, lambda t, upward: pass_on(t, c, upward))

    def far_sum(with_up, with_down):
        total = there(z)
        if with_up:
            total = total + far_up[z].astype(jnp.float32)
        if with_down:
            total = total + far_down[z].astype(jnp.float32)
        far_stage[z] = total.astype(far_stage.dtype)

    def near_sum(c, with_up, with_down):
        total = f32(part, ep, c) + f32(side_in, z, c)
        if with_up:
            total = total + f32(up_in, z, c)
        if with_down:
            total = total + f32(down_in, z, c)
        out_ref[node, :, cols(c)] = total.astype(out_ref.dtype)

    def by_place(add):
        pl.when(has_down & has_up)(lambda: add(True, True))
        pl.when(z == 0)(lambda: add(False, True))
        pl.when(z == line - 1)(lambda: add(True, False))

    pl.when(has_down)(lambda: p_far_up(z).wait_recv())
    pl.when(has_up)(lambda: p_far_down(z).wait_recv())
    by_place(far_sum)
    p_side(z, 0).start()
    for c in order:
        p_side(z, c).wait_recv()
        pl.when(has_down)(lambda: p_up(z, c).wait_recv())
        pl.when(has_up)(lambda: p_down(z, c).wait_recv())
        by_place(lambda with_up, with_down: near_sum(c, with_up, with_down))
        last(c).start()

    def done_far(d, t, upward):
        relay(d, has_down if upward else has_up)(
            lambda: (x_far_down if upward else x_far_up)(t).wait_send()
        )
        (p_far_up if upward else p_far_down)(t).wait_send()

    def done(d, t, c, upward):
        relay(d, has_down if upward else has_up)(
            lambda: (x_down if upward else x_up)(t, c).wait_send()
        )
        if c > 0:
            x_side(t, c).wait_send()
            p_side(t, c).wait_send()
        (p_up if upward else p_down)(t, c).wait_send()

    @pl.when(at_end)
    def _():
        for c in range(pieces):
            x_end(c).wait_send()
        x_far_end().wait_send()

    pl.when(has_up)(lambda: x_far_up(z).wait_send())
    pl.when(has_down)(lambda: x_far_down(z).wait_send())
    for d in range(1, line):
        at_distance(d, lambda t, upward: done_far(d, t, upward))
    for c in range(pieces):
        core_copy(c).wait_send()
        x_side(z, c).wait_send()
        pl.when(has_up)(lambda: x_up(z, c).wait_send())
        pl.when(has_down)(lambda: x_down(z, c).wait_send())
        p_side(z, c).wait_send()
        for d in range(1, line):
            at_distance(d, lambda t, upward: done(d, t, c, upward))
    for c in order:
        last(c).wait_recv()
        last(c).wait_send()


def run_experts(activations, expert_ids, route_scores, capacity, w_gate, w_up, w_down):
    experts = lax.axis_size("node")
    n_ep = lax.axis_size("ep")
    tokens, width = activations.shape
    rows = experts * SEND_CAP
    line = n_ep // SIDE
    hidden = w_gate.shape[1]
    kind = activations.dtype
    count = n_ep * rows
    piece = piece_of(width)
    pieces = width // piece
    vmem = pltpu.VMEM
    sems = pltpu.SemaphoreType.DMA
    here = pl.BlockSpec(memory_space=pltpu.VMEM)
    return pl.pallas_call(
        functools.partial(expert_kernel, line),
        out_shape=(
            jax.ShapeDtypeStruct((experts, rows, width), kind),
            jax.ShapeDtypeStruct((experts * rows, tokens), jnp.bfloat16),
        ),
        in_specs=[pl.BlockSpec(memory_space=pltpu.SMEM)]
        + [here] * 2
        + [pl.BlockSpec(memory_space=pl.ANY)] * 4,
        out_specs=(here, here),
        scratch_shapes=[
            vmem(activations.shape, kind),
            vmem(w_gate.shape, kind),
            vmem(w_up.shape, kind),
            vmem(w_down.shape, kind),
            vmem((count, hidden), jnp.float32),
            vmem((count, hidden), jnp.float32),
            vmem((experts, rows, width), kind),
            vmem((n_ep, rows, width), kind),
            vmem((rows, width), kind),
            vmem((n_ep, rows, width), kind),
        ]
        + [vmem((line, rows, width), kind)] * 4
        + [vmem((line, rows, piece), kind)] * 3
        + [sems((4,)), sems((2, pieces))]
        + [sems((line, pieces))] * 11
        + [sems((pieces,))] * 2
        + [sems((7, line)), sems((pieces + 1,))],
        compiler_params=pltpu.CompilerParams(
            collective_id=0, has_side_effects=True, vmem_limit_bytes=63 * 1024 * 1024
        ),
        cost_estimate=pl.CostEstimate(
            flops=6 * count * width * hidden,
            bytes_accessed=6 * width * hidden,
            transcendentals=count * hidden,
        ),
        name="routed_experts",
    )(capacity, expert_ids.T, route_scores.T, activations, w_gate, w_up, w_down)


def grid_shards(activations, expert_ids, route_scores, capacity, w_gate, w_up, w_down):
    expert_out, combine_w = run_experts(
        activations, expert_ids, route_scores, capacity, w_gate, w_up, w_down
    )
    mixed_out = lax.dot_general(
        combine_w,
        expert_out.reshape(-1, expert_out.shape[2]),
        (((0,), (0,)), ((), ())),
        preferred_element_type=jnp.float32,
    )
    return mixed_out.astype(jnp.bfloat16)


def solution(mesh):
    placed = (
        P(("rep", "node", "ep"), None),
        P(("rep", "node", "ep"), None),
        P(("rep", "node", "ep"), None),
        P(),
        P(None, ("node", "ep")),
        P(None, ("node", "ep")),
        P(("node", "ep"), None),
    )
    fits = mesh.shape["ep"] == SHARDS and mesh.shape["node"] == 2
    return jax.shard_map(
        grid_shards if fits else shards,
        mesh=mesh,
        in_specs=placed,
        out_specs=P(("rep", "node", "ep"), None),
        check_vma=False,
    )
```

```python
import functools

import jax
import jax.numpy as jnp
from jax import lax
from jax.experimental import pallas as pl
from jax.experimental.pallas import tpu as pltpu
from jax.sharding import PartitionSpec as P

MESH = pl.DeviceIdType.MESH
TOPK = 8
SHARDS = 8
SEND_CAP = 8
SIDE = 2


def shards(activations, expert_ids, route_scores, capacity, w_gate, w_up, w_down):
    n_node = lax.axis_size("node")
    n_ep = lax.axis_size("ep")
    window = n_node * (n_ep // SHARDS)
    tok_rows = activations.shape[0]
    model_width = activations.shape[1]
    send_cap = SEND_CAP
    route_weight = (2.5 * route_scores / jnp.sum(route_scores, axis=1, keepdims=True)).astype(
        jnp.bfloat16
    )
    flat_ids = expert_ids.reshape(-1)
    expert_iota = jnp.arange(window, dtype=jnp.int32)
    onehot = (flat_ids[:, None] == expert_iota[None, :]).astype(jnp.int32)
    running = jnp.cumsum(onehot, axis=0)
    ranking = jnp.sum(onehot * running, axis=1) - 1
    limits = jnp.sum(onehot * capacity[:window][None, :], axis=1)
    is_live = (flat_ids < window) & (ranking < limits)
    slot_index = jnp.where(is_live, ranking * window + flat_ids, -1).reshape(tok_rows, TOPK)
    positions = jnp.arange(send_cap * window, dtype=jnp.int32)
    matches = slot_index[:, :, None] == positions[None, None, :]
    select = jnp.any(matches, axis=1).astype(jnp.bfloat16)
    combine_w = jnp.sum(
        jnp.where(matches, route_weight[:, :, None].astype(jnp.float32), 0.0), axis=1
    ).astype(jnp.bfloat16)
    expert_rows = lax.dot_general(
        select, activations, (((0,), (0,)), ((), ())), preferred_element_type=jnp.float32
    ).astype(jnp.bfloat16)
    copies = jnp.broadcast_to(
        expert_rows.reshape(send_cap, window, 1, model_width),
        (send_cap, window, SHARDS, model_width),
    )
    copies = copies.reshape(send_cap, window * SHARDS * model_width)
    received = lax.all_to_all(copies, ("node", "ep"), split_axis=1, concat_axis=0, tiled=True)
    gate_act = jnp.dot(received, w_gate, preferred_element_type=jnp.float32)
    up_act = jnp.dot(received, w_up, preferred_element_type=jnp.float32)
    inner_act = (jax.nn.silu(gate_act) * up_act).astype(jnp.bfloat16)
    partial_value = jnp.dot(inner_act, w_down, preferred_element_type=jnp.float32).astype(
        jnp.bfloat16
    )
    returned = lax.all_to_all(
        partial_value, ("node", "ep"), split_axis=0, concat_axis=1, tiled=True
    )
    summed = jnp.sum(
        returned.reshape(send_cap, window, SHARDS, model_width).astype(jnp.float32), axis=2
    )
    expert_out = summed.astype(jnp.bfloat16).reshape(send_cap * window, model_width)
    mixed_out = jnp.dot(combine_w, expert_out, preferred_element_type=jnp.float32)
    return mixed_out.astype(jnp.bfloat16)


def piece_of(width):
    for size in (1024, 512, 256):
        if width % size == 0:
            return size
    return 128


def select_rows(node, experts, ids_ref, score_ref, cap_ref):
    ids, scores = ids_ref[...], score_ref[...]
    tokens = ids.shape[1]
    slots = experts * SEND_CAP
    weight = (2.5 * scores / jnp.sum(scores, axis=0, keepdims=True)).astype(jnp.bfloat16)
    weight = weight.astype(jnp.float32)
    line = lax.broadcasted_iota(jnp.int32, (experts * slots, tokens), 0)
    rank_of = line % slots - node * SEND_CAP
    hit = jnp.zeros(line.shape, jnp.float32)
    hit_weight = jnp.zeros(line.shape, jnp.float32)
    limit = jnp.zeros(line.shape, jnp.int32)
    for e in range(experts):
        named = ids == e
        here = line // slots == e
        any_named = jnp.sum(jnp.where(named, 1.0, 0.0), axis=0, keepdims=True)
        its_weight = jnp.sum(jnp.where(named, weight, 0.0), axis=0, keepdims=True)
        hit = jnp.where(here, any_named, hit)
        hit_weight = jnp.where(here, its_weight, hit_weight)
        limit = jnp.where(here, cap_ref[e], limit)
    before = lax.broadcasted_iota(jnp.int32, (tokens, tokens), 0) < lax.broadcasted_iota(
        jnp.int32, (tokens, tokens), 1
    )
    rank = jnp.dot(
        hit.astype(jnp.bfloat16),
        jnp.where(before, 1.0, 0.0).astype(jnp.bfloat16),
        preferred_element_type=jnp.float32,
    ).astype(jnp.int32)
    live = (hit > 0.5) & (rank == rank_of) & (rank_of >= 0) & (rank_of < SEND_CAP) & (rank < limit)
    select = jnp.where(live, 1.0, 0.0).astype(jnp.bfloat16)
    return select, jnp.where(live, hit_weight, 0.0).astype(jnp.bfloat16)


def expert_kernel(
    line, cap_ref, ids_ref, score_ref, act_hbm, wg_hbm, wu_hbm, wd_hbm, out_ref, mix_ref,
    act, wg, wu, wd, gate_sum, up_sum, sent, xb, core_in, part,
    side_in, up_in, down_in, stage, far_up, far_down, far_stage,
    w_sem, core_sem, up_sem, down_sem, side_sem, zrecv_sem, yrecv_sem,
    p_side_sem, p_side_recv, p_up_sem, p_up_recv, p_down_sem, p_down_recv, last_sem, last_recv,
    far_sem,
):
    node = lax.axis_index("node")
    ep = lax.axis_index("ep")
    z, y = ep // SIDE, ep % SIDE
    other = 1 - y
    experts, rows, width = sent.shape
    piece = far_stage.shape[2]
    pieces = width // piece
    to_core = {"node": 1 - node}
    to_side = {"ep": z * SIDE + other}
    to_up = {"ep": ep + SIDE}
    to_down = {"ep": ep - SIDE}
    has_up, has_down = z < line - 1, z > 0

    loads = [
        pltpu.make_async_copy(src, dst, w_sem.at[i])
        for i, (src, dst) in enumerate(((act_hbm, act), (wg_hbm, wg), (wu_hbm, wu), (wd_hbm, wd)))
    ]
    loads[0].start()

    barrier = pltpu.get_barrier_semaphore()
    pl.semaphore_signal(barrier, inc=1, device_id=to_core, device_id_type=MESH)
    pl.semaphore_signal(barrier, inc=1, device_id=to_side, device_id_type=MESH)

    @pl.when(has_up)
    def _():
        pl.semaphore_signal(barrier, inc=1, device_id=to_up, device_id_type=MESH)

    @pl.when(has_down)
    def _():
        pl.semaphore_signal(barrier, inc=1, device_id=to_down, device_id_type=MESH)

    def cols(c):
        return pl.ds(c * piece, piece)

    def remote(src, dst, send, recv, where):
        return pltpu.make_async_remote_copy(
            src_ref=src, dst_ref=dst, send_sem=send, recv_sem=recv,
            device_id=where, device_id_type=MESH,
        )

    def core_copy(c):
        return remote(
            sent.at[1 - node, :, cols(c)], core_in.at[:, cols(c)],
            core_sem.at[0, c], core_sem.at[1, c], to_core,
        )

    def x_copy(o, c, send, recv, where):
        ref = xb.at[o * SIDE + y, :, cols(c)]
        return remote(ref, ref, send.at[o, c], recv.at[o, c], where)

    def x_up(o, c):
        return x_copy(o, c, up_sem, zrecv_sem, to_up)

    def x_down(o, c):
        return x_copy(o, c, down_sem, zrecv_sem, to_down)

    def x_side(o, c):
        return x_copy(o, c, side_sem, yrecv_sem, to_side)

    def far(o, i, where):
        ref = xb.at[o * SIDE + other, :, cols(0)]
        return remote(ref, ref, far_sem.at[i, o], far_sem.at[2, o], where)

    def x_far_up(o):
        return far(o, 0, to_up)

    def x_far_down(o):
        return far(o, 1, to_down)

    select, mix = select_rows(node, experts, ids_ref, score_ref, cap_ref)
    mix_ref[...] = mix
    loads[0].wait()
    for load in loads[1:]:
        load.start()
    for c in range(pieces):
        taken = jnp.dot(select, act[:, cols(c)], preferred_element_type=jnp.float32)
        sent[:, :, cols(c)] = taken.astype(sent.dtype).reshape(experts, rows, piece)
        if c == 0:
            pl.semaphore_wait(barrier, 2 + has_up.astype(jnp.int32) + has_down.astype(jnp.int32))
        core_copy(c).start()
    for c in range(pieces):
        core_copy(c).wait_recv()
        xb[ep, :, cols(c)] = sent[node, :, cols(c)] + core_in[:, cols(c)]
        x_side(z, c).start()
        pl.when(has_up)(lambda: x_up(z, c).start())
        pl.when(has_down)(lambda: x_down(z, c).start())

    x_side(z, 0).wait_recv()
    pl.when(has_up)(lambda: x_far_up(z).start())
    pl.when(has_down)(lambda: x_far_down(z).start())

    for d in range(1, line):
        for c in range(pieces):
            @pl.when(z - d >= 0)
            def _():
                x_up(z - d, c).wait_recv()
                pl.when(has_up)(lambda: x_up(z - d, c).start())
                if c > 0:
                    x_side(z - d, c).start()

            @pl.when(z + d < line)
            def _():
                x_down(z + d, c).wait_recv()
                pl.when(has_down)(lambda: x_down(z + d, c).start())
                if c > 0:
                    x_side(z + d, c).start()

        @pl.when(z - d >= 0)
        def _():
            x_far_up(z - d).wait_recv()
            pl.when(has_up)(lambda: x_far_up(z - d).start())

        @pl.when(z + d < line)
        def _():
            x_far_down(z + d).wait_recv()
            pl.when(has_down)(lambda: x_far_down(z + d).start())

    count = xb.shape[0] * rows
    loads[1].wait()
    loads[2].wait()
    for c in range(pieces):
        if c > 0:
            for o in range(line):
                x_side(o, c).wait_recv()
        x = xb[:, :, cols(c)].reshape(count, piece)
        gate_part = jnp.dot(x, wg[cols(c), :], preferred_element_type=jnp.float32)
        up_part = jnp.dot(x, wu[cols(c), :], preferred_element_type=jnp.float32)
        if c == 0:
            gate_sum[...] = gate_part
            up_sum[...] = up_part
        else:
            gate_sum[...] += gate_part
            up_sum[...] += up_part

    gate = gate_sum[...]
    inner = (gate / (1.0 + jnp.exp(-gate)) * up_sum[...]).astype(jnp.bfloat16)
    loads[3].wait()

    def p_side(t, c):
        src = far_stage.at[t] if c == 0 else part.at[t * SIDE + other, :, cols(c)]
        return remote(
            src, side_in.at[t, :, cols(c)],
            p_side_sem.at[t, c], p_side_recv.at[t, c], to_side,
        )

    def p_up(t, c):
        return remote(
            stage.at[t, :, cols(c)], up_in.at[t, :, cols(c)],
            p_up_sem.at[t, c], p_up_recv.at[t, c], to_up,
        )

    def p_down(t, c):
        return remote(
            stage.at[t, :, cols(c)], down_in.at[t, :, cols(c)],
            p_down_sem.at[t, c], p_down_recv.at[t, c], to_down,
        )

    def p_far_up(t):
        return remote(far_stage.at[t], far_up.at[t], far_sem.at[3, t], far_sem.at[4, t], to_up)

    def p_far_down(t):
        return remote(far_stage.at[t], far_down.at[t], far_sem.at[5, t], far_sem.at[6, t], to_down)

    def last(c):
        ref = out_ref.at[node, :, cols(c)]
        return remote(ref, ref, last_sem.at[c], last_recv.at[c], to_core)

    def at_distance(d, act):
        pl.when(z + d < line)(lambda: act(z + d, True))
        pl.when(z - d >= 0)(lambda: act(z - d, False))

    def f32(ref, t, c):
        return ref[t, :, cols(c)].astype(jnp.float32)

    def here(t, c):
        own = f32(part, t * SIDE + y, c)
        return own if c == 0 else own + f32(side_in, t, c)

    def there(t):
        return f32(part, t * SIDE + other, 0)

    def pass_on(t, c, upward):
        if c > 0:
            p_side(t, c).wait_recv()
        copy, arrived = (p_up, up_in) if upward else (p_down, down_in)
        more, end = (has_down, z == 0) if upward else (has_up, z == line - 1)

        @pl.when(more)
        def _():
            copy(t, c).wait_recv()
            stage[t, :, cols(c)] = (here(t, c) + f32(arrived, t, c)).astype(stage.dtype)

        @pl.when(end)
        def _():
            stage[t, :, cols(c)] = here(t, c).astype(stage.dtype)

        copy(t, c).start()

    def pass_far(t, upward):
        copy, arrived = (p_far_up, far_up) if upward else (p_far_down, far_down)
        more, end = (has_down, z == 0) if upward else (has_up, z == line - 1)

        @pl.when(more)
        def _():
            copy(t).wait_recv()
            far_stage[t] = (there(t) + arrived[t].astype(jnp.float32)).astype(far_stage.dtype)

        @pl.when(end)
        def _():
            far_stage[t] = there(t).astype(far_stage.dtype)

        copy(t).start()

    order = list(range(1, pieces)) + [0]
    for c in order:
        value = jnp.dot(inner, wd[:, cols(c)], preferred_element_type=jnp.float32)
        part[:, :, cols(c)] = value.astype(part.dtype).reshape(part.shape[0], rows, piece)
        if c > 0:
            at_distance(line - 1, lambda t, upward: p_side(t, c).start())
            if line > 2:
                at_distance(line - 2, lambda t, upward: p_side(t, c).start())
    for d in range(line - 3, 0, -1):
        for c in range(1, pieces):
            at_distance(d, lambda t, upward: p_side(t, c).start())
    for c in range(1, pieces):
        p_side(z, c).start()

    for d in range(line - 1, 0, -1):
        at_distance(d, lambda t, upward: pass_on(t, 0, upward))
        at_distance(d, pass_far)
        for c in range(1, pieces):
            at_distance(d, lambda t, upward: pass_on(t, c, upward))

    def far_sum(with_up, with_down):
        total = there(z)
        if with_up:
            total = total + far_up[z].astype(jnp.float32)
        if with_down:
            total = total + far_down[z].astype(jnp.float32)
        far_stage[z] = total.astype(far_stage.dtype)

    def near_sum(c, with_up, with_down):
        total = f32(part, ep, c) + f32(side_in, z, c)
        if with_up:
            total = total + f32(up_in, z, c)
        if with_down:
            total = total + f32(down_in, z, c)
        out_ref[node, :, cols(c)] = total.astype(out_ref.dtype)

    def by_place(add):
        pl.when(has_down & has_up)(lambda: add(True, True))
        pl.when(z == 0)(lambda: add(False, True))
        pl.when(z == line - 1)(lambda: add(True, False))

    pl.when(has_down)(lambda: p_far_up(z).wait_recv())
    pl.when(has_up)(lambda: p_far_down(z).wait_recv())
    by_place(far_sum)
    p_side(z, 0).start()
    for c in order:
        p_side(z, c).wait_recv()
        pl.when(has_down)(lambda: p_up(z, c).wait_recv())
        pl.when(has_up)(lambda: p_down(z, c).wait_recv())
        by_place(lambda with_up, with_down: near_sum(c, with_up, with_down))
        last(c).start()

    def done_far(t, upward):
        pl.when(has_down if upward else has_up)(
            lambda: (x_far_down if upward else x_far_up)(t).wait_send()
        )
        (p_far_up if upward else p_far_down)(t).wait_send()

    def done(t, c, upward):
        pl.when(has_down if upward else has_up)(
            lambda: (x_down if upward else x_up)(t, c).wait_send()
        )
        if c > 0:
            x_side(t, c).wait_send()
            p_side(t, c).wait_send()
        (p_up if upward else p_down)(t, c).wait_send()

    pl.when(has_up)(lambda: x_far_up(z).wait_send())
    pl.when(has_down)(lambda: x_far_down(z).wait_send())
    for d in range(1, line):
        at_distance(d, done_far)
    for c in range(pieces):
        core_copy(c).wait_send()
        x_side(z, c).wait_send()
        pl.when(has_up)(lambda: x_up(z, c).wait_send())
        pl.when(has_down)(lambda: x_down(z, c).wait_send())
        p_side(z, c).wait_send()
        for d in range(1, line):
            at_distance(d, lambda t, upward: done(t, c, upward))
    for c in order:
        last(c).wait_recv()
        last(c).wait_send()


def run_experts(activations, expert_ids, route_scores, capacity, w_gate, w_up, w_down):
    experts = lax.axis_size("node")
    n_ep = lax.axis_size("ep")
    tokens, width = activations.shape
    rows = experts * SEND_CAP
    line = n_ep // SIDE
    hidden = w_gate.shape[1]
    kind = activations.dtype
    count = n_ep * rows
    piece = piece_of(width)
    pieces = width // piece
    vmem = pltpu.VMEM
    sems = pltpu.SemaphoreType.DMA
    here = pl.BlockSpec(memory_space=pltpu.VMEM)
    return pl.pallas_call(
        functools.partial(expert_kernel, line),
        out_shape=(
            jax.ShapeDtypeStruct((experts, rows, width), kind),
            jax.ShapeDtypeStruct((experts * rows, tokens), jnp.bfloat16),
        ),
        in_specs=[pl.BlockSpec(memory_space=pltpu.SMEM)]
        + [here] * 2
        + [pl.BlockSpec(memory_space=pl.ANY)] * 4,
        out_specs=(here, here),
        scratch_shapes=[
            vmem(activations.shape, kind),
            vmem(w_gate.shape, kind),
            vmem(w_up.shape, kind),
            vmem(w_down.shape, kind),
            vmem((count, hidden), jnp.float32),
            vmem((count, hidden), jnp.float32),
            vmem((experts, rows, width), kind),
            vmem((n_ep, rows, width), kind),
            vmem((rows, width), kind),
            vmem((n_ep, rows, width), kind),
        ]
        + [vmem((line, rows, width), kind)] * 4
        + [vmem((line, rows, piece), kind)] * 3
        + [sems((4,)), sems((2, pieces))]
        + [sems((line, pieces))] * 11
        + [sems((pieces,))] * 2
        + [sems((7, line))],
        compiler_params=pltpu.CompilerParams(
            collective_id=0, has_side_effects=True, vmem_limit_bytes=62 * 1024 * 1024 + 400 * 1024
        ),
        cost_estimate=pl.CostEstimate(
            flops=6 * count * width * hidden,
            bytes_accessed=6 * width * hidden,
            transcendentals=count * hidden,
        ),
        name="routed_experts",
    )(capacity, expert_ids.T, route_scores.T, activations, w_gate, w_up, w_down)


def grid_shards(activations, expert_ids, route_scores, capacity, w_gate, w_up, w_down):
    expert_out, combine_w = run_experts(
        activations, expert_ids, route_scores, capacity, w_gate, w_up, w_down
    )
    mixed_out = lax.dot_general(
        combine_w,
        expert_out.reshape(-1, expert_out.shape[2]),
        (((0,), (0,)), ((), ())),
        preferred_element_type=jnp.float32,
    )
    return mixed_out.astype(jnp.bfloat16)


def solution(mesh):
    placed = (
        P(("rep", "node", "ep"), None),
        P(("rep", "node", "ep"), None),
        P(("rep", "node", "ep"), None),
        P(),
        P(None, ("node", "ep")),
        P(None, ("node", "ep")),
        P(("node", "ep"), None),
    )
    fits = mesh.shape["ep"] == SHARDS and mesh.shape["node"] == 2
    return jax.shard_map(
        grid_shards if fits else shards,
        mesh=mesh,
        in_specs=placed,
        out_specs=P(("rep", "node", "ep"), None),
        check_vma=False,
    )
```

```python
import functools

import jax
import jax.numpy as jnp
from jax import lax
from jax.experimental import pallas as pl
from jax.experimental.pallas import tpu as pltpu
from jax.sharding import PartitionSpec as P

MESH = pl.DeviceIdType.MESH
TOPK = 8
SHARDS = 8
SEND_CAP = 8
SIDE = 2


def shards(activations, expert_ids, route_scores, capacity, w_gate, w_up, w_down):
    n_node = lax.axis_size("node")
    n_ep = lax.axis_size("ep")
    window = n_node * (n_ep // SHARDS)
    tok_rows = activations.shape[0]
    model_width = activations.shape[1]
    send_cap = SEND_CAP
    route_weight = (2.5 * route_scores / jnp.sum(route_scores, axis=1, keepdims=True)).astype(
        jnp.bfloat16
    )
    flat_ids = expert_ids.reshape(-1)
    expert_iota = jnp.arange(window, dtype=jnp.int32)
    onehot = (flat_ids[:, None] == expert_iota[None, :]).astype(jnp.int32)
    running = jnp.cumsum(onehot, axis=0)
    ranking = jnp.sum(onehot * running, axis=1) - 1
    limits = jnp.sum(onehot * capacity[:window][None, :], axis=1)
    is_live = (flat_ids < window) & (ranking < limits)
    slot_index = jnp.where(is_live, ranking * window + flat_ids, -1).reshape(tok_rows, TOPK)
    positions = jnp.arange(send_cap * window, dtype=jnp.int32)
    matches = slot_index[:, :, None] == positions[None, None, :]
    select = jnp.any(matches, axis=1).astype(jnp.bfloat16)
    combine_w = jnp.sum(
        jnp.where(matches, route_weight[:, :, None].astype(jnp.float32), 0.0), axis=1
    ).astype(jnp.bfloat16)
    expert_rows = lax.dot_general(
        select, activations, (((0,), (0,)), ((), ())), preferred_element_type=jnp.float32
    ).astype(jnp.bfloat16)
    copies = jnp.broadcast_to(
        expert_rows.reshape(send_cap, window, 1, model_width),
        (send_cap, window, SHARDS, model_width),
    )
    copies = copies.reshape(send_cap, window * SHARDS * model_width)
    received = lax.all_to_all(copies, ("node", "ep"), split_axis=1, concat_axis=0, tiled=True)
    gate_act = jnp.dot(received, w_gate, preferred_element_type=jnp.float32)
    up_act = jnp.dot(received, w_up, preferred_element_type=jnp.float32)
    inner_act = (jax.nn.silu(gate_act) * up_act).astype(jnp.bfloat16)
    partial_value = jnp.dot(inner_act, w_down, preferred_element_type=jnp.float32).astype(
        jnp.bfloat16
    )
    returned = lax.all_to_all(
        partial_value, ("node", "ep"), split_axis=0, concat_axis=1, tiled=True
    )
    summed = jnp.sum(
        returned.reshape(send_cap, window, SHARDS, model_width).astype(jnp.float32), axis=2
    )
    expert_out = summed.astype(jnp.bfloat16).reshape(send_cap * window, model_width)
    mixed_out = jnp.dot(combine_w, expert_out, preferred_element_type=jnp.float32)
    return mixed_out.astype(jnp.bfloat16)


def piece_of(width):
    for size in (1024, 512, 256):
        if width % size == 0:
            return size
    return 128


def select_rows(node, experts, ids_ref, score_ref, cap_ref):
    ids, scores = ids_ref[...], score_ref[...]
    tokens = ids.shape[1]
    slots = experts * SEND_CAP
    weight = (2.5 * scores / jnp.sum(scores, axis=0, keepdims=True)).astype(jnp.bfloat16)
    weight = weight.astype(jnp.float32)
    line = lax.broadcasted_iota(jnp.int32, (experts * slots, tokens), 0)
    rank_of = line % slots - node * SEND_CAP
    hit = jnp.zeros(line.shape, jnp.float32)
    hit_weight = jnp.zeros(line.shape, jnp.float32)
    limit = jnp.zeros(line.shape, jnp.int32)
    for e in range(experts):
        named = ids == e
        here = line // slots == e
        any_named = jnp.sum(jnp.where(named, 1.0, 0.0), axis=0, keepdims=True)
        its_weight = jnp.sum(jnp.where(named, weight, 0.0), axis=0, keepdims=True)
        hit = jnp.where(here, any_named, hit)
        hit_weight = jnp.where(here, its_weight, hit_weight)
        limit = jnp.where(here, cap_ref[e], limit)
    before = lax.broadcasted_iota(jnp.int32, (tokens, tokens), 0) < lax.broadcasted_iota(
        jnp.int32, (tokens, tokens), 1
    )
    rank = jnp.dot(
        hit.astype(jnp.bfloat16),
        jnp.where(before, 1.0, 0.0).astype(jnp.bfloat16),
        preferred_element_type=jnp.float32,
    ).astype(jnp.int32)
    live = (hit > 0.5) & (rank == rank_of) & (rank_of >= 0) & (rank_of < SEND_CAP) & (rank < limit)
    select = jnp.where(live, 1.0, 0.0).astype(jnp.bfloat16)
    return select, jnp.where(live, hit_weight, 0.0).astype(jnp.bfloat16)


def expert_kernel(
    line, cap_ref, ids_ref, score_ref, act_hbm, wg_hbm, wu_hbm, wd_hbm, out_ref, mix_ref,
    act, wg, wu, wd, gate_sum, up_sum, sent, xb, core_in, part,
    side_in, up_in, down_in, stage, far_up, far_down, far_stage,
    w_sem, core_sem, up_sem, down_sem, side_sem, zrecv_sem, yrecv_sem,
    p_side_sem, p_side_recv, p_up_sem, p_up_recv, p_down_sem, p_down_recv, last_sem, last_recv,
    far_sem, near_sem, near_in, near_stage,
):
    node = lax.axis_index("node")
    ep = lax.axis_index("ep")
    z, y = ep // SIDE, ep % SIDE
    other = 1 - y
    experts, rows, width = sent.shape
    piece = far_stage.shape[2]
    pieces = width // piece
    to_core = {"node": 1 - node}
    to_side = {"ep": z * SIDE + other}
    to_up = {"ep": ep + SIDE}
    to_down = {"ep": ep - SIDE}
    has_up, has_down = z < line - 1, z > 0
    at_end = (z == 0) | (z == line - 1)
    blocks = xb.shape[0] // 2
    half = z // (line // 2)
    near = z + 1 - 2 * (z % 2)
    to_near = {"ep": near * SIDE + y}
    far_end, far_mid = (1 - half) * (line - 1), line // 2 - half

    loads = [
        pltpu.make_async_copy(src, dst, w_sem.at[i])
        for i, (src, dst) in enumerate(((act_hbm, act), (wg_hbm, wg), (wu_hbm, wu), (wd_hbm, wd)))
    ]
    loads[0].start()

    barrier = pltpu.get_barrier_semaphore()
    pl.semaphore_signal(barrier, inc=1, device_id=to_core, device_id_type=MESH)
    pl.semaphore_signal(barrier, inc=1, device_id=to_side, device_id_type=MESH)

    @pl.when(has_up)
    def _():
        pl.semaphore_signal(barrier, inc=1, device_id=to_up, device_id_type=MESH)

    @pl.when(has_down)
    def _():
        pl.semaphore_signal(barrier, inc=1, device_id=to_down, device_id_type=MESH)

    def cols(c):
        return pl.ds(c * piece, piece)

    def remote(src, dst, send, recv, where):
        return pltpu.make_async_remote_copy(
            src_ref=src, dst_ref=dst, send_sem=send, recv_sem=recv,
            device_id=where, device_id_type=MESH,
        )

    def core_copy(c):
        return remote(
            sent.at[1 - node, :, cols(c)], core_in.at[:, cols(c)],
            core_sem.at[0, c], core_sem.at[1, c], to_core,
        )

    def x_copy(o, c, send, recv, where):
        ref = xb.at[o * SIDE + y, :, cols(c)]
        return remote(ref, ref, send.at[o, c], recv.at[o, c], where)

    def x_up(o, c):
        return x_copy(o, c, up_sem, zrecv_sem, to_up)

    def x_down(o, c):
        return x_copy(o, c, down_sem, zrecv_sem, to_down)

    def x_side(o, c):
        return x_copy(o, c, side_sem, yrecv_sem, to_side)

    def far(o, i, where):
        ref = xb.at[o * SIDE + other, :, cols(0)]
        return remote(ref, ref, far_sem.at[i, o], far_sem.at[2, o], where)

    def x_far_up(o):
        return far(o, 0, to_up)

    def x_far_down(o):
        return far(o, 1, to_down)

    select, mix = select_rows(node, experts, ids_ref, score_ref, cap_ref)
    mix_ref[...] = mix
    loads[0].wait()
    for load in loads[1:]:
        load.start()
    for c in range(pieces):
        taken = jnp.dot(select, act[:, cols(c)], preferred_element_type=jnp.float32)
        sent[:, :, cols(c)] = taken.astype(sent.dtype).reshape(experts, rows, piece)
        if c == 0:
            pl.semaphore_wait(barrier, 2 + has_up.astype(jnp.int32) + has_down.astype(jnp.int32))
        core_copy(c).start()
    for c in range(pieces):
        core_copy(c).wait_recv()
        xb[ep, :, cols(c)] = sent[node, :, cols(c)] + core_in[:, cols(c)]
        x_side(z, c).start()
        pl.when(has_up)(lambda: x_up(z, c).start())
        pl.when(has_down)(lambda: x_down(z, c).start())

    x_side(z, 0).wait_recv()
    pl.when(has_up)(lambda: x_far_up(z).start())
    pl.when(has_down)(lambda: x_far_down(z).start())

    def p_side(t, c, own=False):
        src = part.at[t * SIDE + other, :, cols(c)]
        if own:
            src = far_stage.at[t] if c == 0 else near_stage.at[:, cols(c)]
        return remote(
            src, side_in.at[t, :, cols(c)],
            p_side_sem.at[t, c], p_side_recv.at[t, c], to_side,
        )

    def p_up(t, c):
        return remote(
            stage.at[t, :, cols(c)], up_in.at[t, :, cols(c)],
            p_up_sem.at[t, c], p_up_recv.at[t, c], to_up,
        )

    def p_down(t, c):
        return remote(
            stage.at[t, :, cols(c)], down_in.at[t, :, cols(c)],
            p_down_sem.at[t, c], p_down_recv.at[t, c], to_down,
        )

    def p_far_up(t):
        return remote(far_stage.at[t], far_up.at[t], far_sem.at[3, t], far_sem.at[4, t], to_up)

    def p_far_down(t):
        return remote(far_stage.at[t], far_down.at[t], far_sem.at[5, t], far_sem.at[6, t], to_down)

    def p_near(c):
        return remote(
            part.at[near * SIDE + other, :, cols(c)], near_in.at[:, cols(c)],
            near_sem.at[0, c], near_sem.at[1, c], to_near,
        )

    def last(c):
        ref = out_ref.at[node, :, cols(c)]
        return remote(ref, ref, last_sem.at[c], last_recv.at[c], to_core)

    def at_distance(d, act):
        pl.when(z + d < line)(lambda: act(z + d, True))
        pl.when(z - d >= 0)(lambda: act(z - d, False))

    def f32(ref, t, c):
        return ref[t, :, cols(c)].astype(jnp.float32)

    def there(t):
        return f32(part, t * SIDE + other, 0)

    def pass_on(t, c, upward, across):
        across = across and c > 0
        if across:
            p_side(t, c).wait_recv()
        copy, arrived = (p_up, up_in) if upward else (p_down, down_in)
        more, end = (has_down, z == 0) if upward else (has_up, z == line - 1)

        def here():
            own = f32(part, t * SIDE + y, c)
            return own + f32(side_in, t, c) if across else own

        @pl.when(more)
        def _():
            copy(t, c).wait_recv()
            stage[t, :, cols(c)] = (here() + f32(arrived, t, c)).astype(stage.dtype)

        @pl.when(end)
        def _():
            stage[t, :, cols(c)] = here().astype(stage.dtype)

        copy(t, c).start()

    def pass_far(t, upward):
        copy, arrived = (p_far_up, far_up) if upward else (p_far_down, far_down)
        more, end = (has_down, z == 0) if upward else (has_up, z == line - 1)

        @pl.when(more)
        def _():
            copy(t).wait_recv()
            far_stage[t] = (there(t) + arrived[t].astype(jnp.float32)).astype(far_stage.dtype)

        @pl.when(end)
        def _():
            far_stage[t] = there(t).astype(far_stage.dtype)

        copy(t).start()

    def add_gate_up(start, c):
        x = xb[pl.ds(start, blocks), :, cols(c)].reshape(blocks * rows, piece)
        gate_part = jnp.dot(x, wg[cols(c), :], preferred_element_type=jnp.float32)
        up_part = jnp.dot(x, wu[cols(c), :], preferred_element_type=jnp.float32)
        if c == 0:
            gate_sum[...] = gate_part
            up_sum[...] = up_part
        else:
            gate_sum[...] += gate_part
            up_sum[...] += up_part

    def swiglu():
        gate = gate_sum[...]
        return (gate / (1.0 + jnp.exp(-gate)) * up_sum[...]).astype(jnp.bfloat16)

    def put_partial(inner, start, c):
        value = jnp.dot(inner, wd[:, cols(c)], preferred_element_type=jnp.float32)
        part[pl.ds(start, blocks), :, cols(c)] = value.astype(part.dtype).reshape(
            blocks, rows, piece
        )

    def send_near(c):
        if c > 0:
            p_near(c).start()

        @pl.when(z == 0)
        def _():
            pass_on(z + 1, c, True, False)
            if c == 0:
                pass_far(z + 1, True)

        @pl.when(z == line - 1)
        def _():
            pass_on(z - 1, c, False, False)
            if c == 0:
                pass_far(z - 1, False)

    inner = None
    for d in range(1, line):
        if d == line - 1:
            inner = swiglu()
            loads[3].wait()
        for c in range(pieces):
            @pl.when(z - d >= 0)
            def _():
                x_up(z - d, c).wait_recv()
                pl.when(has_up)(lambda: x_up(z - d, c).start())
                if c > 0:
                    x_side(z - d, c).start()

            @pl.when(z + d < line)
            def _():
                x_down(z + d, c).wait_recv()
                pl.when(has_down)(lambda: x_down(z + d, c).start())
                if c > 0:
                    x_side(z + d, c).start()

            if d == line - 2:
                if c == 0:
                    loads[1].wait()
                    loads[2].wait()
                else:
                    x_side(z, c).wait_recv()
                    x_side(near, c).wait_recv()
                add_gate_up(half * blocks, c)
            if d == line - 1:
                put_partial(inner, half * blocks, c)
                pl.when(at_end)(lambda: send_near(c))

        @pl.when(z - d >= 0)
        def _():
            x_far_up(z - d).wait_recv()
            pl.when(has_up)(lambda: x_far_up(z - d).start())

        @pl.when(z + d < line)
        def _():
            x_far_down(z + d).wait_recv()
            pl.when(has_down)(lambda: x_far_down(z + d).start())

    for c in range(pieces):
        if c > 0:
            x_side(far_end, c).wait_recv()
            x_side(far_mid, c).wait_recv()
        add_gate_up((1 - half) * blocks, c)
    inner = swiglu()

    order = list(range(1, pieces)) + [0]
    for c in order:
        put_partial(inner, (1 - half) * blocks, c)
        if c > 0:
            p_side(far_end, c).start()

            @pl.when(jnp.logical_not(at_end))
            def _():
                p_near(c).start()

    for c in range(1, pieces):
        p_side(far_mid, c).start()

    for d in range(line - 1, 1, -1):
        at_distance(d, lambda t, upward: pass_on(t, 0, upward, True))
        at_distance(d, pass_far)
        for c in range(1, pieces):
            at_distance(d, lambda t, upward: pass_on(t, c, upward, True))
        if d == line - 1:
            for c in range(1, pieces):
                p_near(c).wait_recv()
                total = f32(part, z * SIDE + other, c) + near_in[:, cols(c)].astype(jnp.float32)
                near_stage[:, cols(c)] = total.astype(near_stage.dtype)
                p_side(z, c, True).start()

    @pl.when(z == line // 2 - 1)
    def _():
        pass_on(z - 1, 0, False, False)
        pass_far(z - 1, False)
        pass_on(z + 1, 0, True, True)
        pass_far(z + 1, True)
        for c in range(1, pieces):
            pass_on(z - 1, c, False, False)
        for c in range(1, pieces):
            pass_on(z + 1, c, True, True)

    @pl.when(z == line // 2)
    def _():
        pass_on(z + 1, 0, True, False)
        pass_far(z + 1, True)
        pass_on(z - 1, 0, False, True)
        pass_far(z - 1, False)
        for c in range(1, pieces):
            pass_on(z + 1, c, True, False)
        for c in range(1, pieces):
            pass_on(z - 1, c, False, True)

    def far_sum(with_up, with_down):
        total = there(z)
        if with_up:
            total = total + far_up[z].astype(jnp.float32)
        if with_down:
            total = total + far_down[z].astype(jnp.float32)
        far_stage[z] = total.astype(far_stage.dtype)

    def finish(c, with_up, with_down):
        total = f32(part, ep, c) + f32(side_in, z, c)
        if with_up:
            total = total + f32(up_in, z, c)
        if with_down:
            total = total + f32(down_in, z, c)
        out_ref[node, :, cols(c)] = total.astype(out_ref.dtype)

    def by_place(add):
        pl.when(has_down & has_up)(lambda: add(True, True))
        pl.when(z == 0)(lambda: add(False, True))
        pl.when(z == line - 1)(lambda: add(True, False))

    pl.when(has_down)(lambda: p_far_up(z).wait_recv())
    pl.when(has_up)(lambda: p_far_down(z).wait_recv())
    by_place(far_sum)
    p_side(z, 0, True).start()
    for c in order:
        p_side(z, c, True).wait_recv()
        pl.when(has_down)(lambda: p_up(z, c).wait_recv())
        pl.when(has_up)(lambda: p_down(z, c).wait_recv())
        by_place(lambda with_up, with_down: finish(c, with_up, with_down))
        last(c).start()

    def done_far(t, upward):
        pl.when(has_down if upward else has_up)(
            lambda: (x_far_down if upward else x_far_up)(t).wait_send()
        )
        (p_far_up if upward else p_far_down)(t).wait_send()

    def done(t, c, upward):
        pl.when(has_down if upward else has_up)(
            lambda: (x_down if upward else x_up)(t, c).wait_send()
        )
        if c > 0:
            x_side(t, c).wait_send()
        (p_up if upward else p_down)(t, c).wait_send()

    pl.when(has_up)(lambda: x_far_up(z).wait_send())
    pl.when(has_down)(lambda: x_far_down(z).wait_send())
    for d in range(1, line):
        at_distance(d, done_far)
    for c in range(pieces):
        core_copy(c).wait_send()
        x_side(z, c).wait_send()
        pl.when(has_up)(lambda: x_up(z, c).wait_send())
        pl.when(has_down)(lambda: x_down(z, c).wait_send())
        p_side(z, c, True).wait_send()
        if c > 0:
            p_near(c).wait_send()
            p_side(far_end, c).wait_send()
            p_side(far_mid, c).wait_send()
        for d in range(1, line):
            at_distance(d, lambda t, upward: done(t, c, upward))
    for c in order:
        last(c).wait_recv()
        last(c).wait_send()


def run_experts(activations, expert_ids, route_scores, capacity, w_gate, w_up, w_down):
    experts = lax.axis_size("node")
    n_ep = lax.axis_size("ep")
    tokens, width = activations.shape
    rows = experts * SEND_CAP
    line = n_ep // SIDE
    hidden = w_gate.shape[1]
    kind = activations.dtype
    count = n_ep * rows
    piece = piece_of(width)
    pieces = width // piece
    vmem = pltpu.VMEM
    sems = pltpu.SemaphoreType.DMA
    here = pl.BlockSpec(memory_space=pltpu.VMEM)
    return pl.pallas_call(
        functools.partial(expert_kernel, line),
        out_shape=(
            jax.ShapeDtypeStruct((experts, rows, width), kind),
            jax.ShapeDtypeStruct((experts * rows, tokens), jnp.bfloat16),
        ),
        in_specs=[pl.BlockSpec(memory_space=pltpu.SMEM)]
        + [here] * 2
        + [pl.BlockSpec(memory_space=pl.ANY)] * 4,
        out_specs=(here, here),
        scratch_shapes=[
            vmem(activations.shape, kind),
            vmem(w_gate.shape, kind),
            vmem(w_up.shape, kind),
            vmem(w_down.shape, kind),
            vmem((count // 2, hidden), jnp.float32),
            vmem((count // 2, hidden), jnp.float32),
            vmem((experts, rows, width), kind),
            vmem((n_ep, rows, width), kind),
            vmem((rows, width), kind),
            vmem((n_ep, rows, width), kind),
        ]
        + [vmem((line, rows, width), kind)] * 4
        + [vmem((line, rows, piece), kind)] * 3
        + [sems((4,)), sems((2, pieces))]
        + [sems((line, pieces))] * 11
        + [sems((pieces,))] * 2
        + [sems((7, line)), sems((2, pieces)), vmem((rows, width), kind), vmem((rows, width), kind)],
        compiler_params=pltpu.CompilerParams(
            collective_id=0, has_side_effects=True, vmem_limit_bytes=62 * 1024 * 1024 + 400 * 1024
        ),
        cost_estimate=pl.CostEstimate(
            flops=6 * count * width * hidden,
            bytes_accessed=6 * width * hidden,
            transcendentals=count * hidden,
        ),
        name="routed_experts",
    )(capacity, expert_ids.T, route_scores.T, activations, w_gate, w_up, w_down)


def grid_shards(activations, expert_ids, route_scores, capacity, w_gate, w_up, w_down):
    expert_out, combine_w = run_experts(
        activations, expert_ids, route_scores, capacity, w_gate, w_up, w_down
    )
    mixed_out = lax.dot_general(
        combine_w,
        expert_out.reshape(-1, expert_out.shape[2]),
        (((0,), (0,)), ((), ())),
        preferred_element_type=jnp.float32,
    )
    return mixed_out.astype(jnp.bfloat16)


def solution(mesh):
    placed = (
        P(("rep", "node", "ep"), None),
        P(("rep", "node", "ep"), None),
        P(("rep", "node", "ep"), None),
        P(),
        P(None, ("node", "ep")),
        P(None, ("node", "ep")),
        P(("node", "ep"), None),
    )
    fits = mesh.shape["ep"] == SHARDS and mesh.shape["node"] == 2
    return jax.shard_map(
        grid_shards if fits else shards,
        mesh=mesh,
        in_specs=placed,
        out_specs=P(("rep", "node", "ep"), None),
        check_vma=False,
    )
```

```python
import functools

import jax
import jax.numpy as jnp
from jax import lax
from jax.experimental import pallas as pl
from jax.experimental.pallas import tpu as pltpu
from jax.sharding import PartitionSpec as P

MESH = pl.DeviceIdType.MESH
TOPK = 8
SHARDS = 8
SEND_CAP = 8
SIDE = 2


def shards(activations, expert_ids, route_scores, capacity, w_gate, w_up, w_down):
    n_node = lax.axis_size("node")
    n_ep = lax.axis_size("ep")
    window = n_node * (n_ep // SHARDS)
    tok_rows = activations.shape[0]
    model_width = activations.shape[1]
    send_cap = SEND_CAP
    route_weight = (2.5 * route_scores / jnp.sum(route_scores, axis=1, keepdims=True)).astype(
        jnp.bfloat16
    )
    flat_ids = expert_ids.reshape(-1)
    expert_iota = jnp.arange(window, dtype=jnp.int32)
    onehot = (flat_ids[:, None] == expert_iota[None, :]).astype(jnp.int32)
    running = jnp.cumsum(onehot, axis=0)
    ranking = jnp.sum(onehot * running, axis=1) - 1
    limits = jnp.sum(onehot * capacity[:window][None, :], axis=1)
    is_live = (flat_ids < window) & (ranking < limits)
    slot_index = jnp.where(is_live, ranking * window + flat_ids, -1).reshape(tok_rows, TOPK)
    positions = jnp.arange(send_cap * window, dtype=jnp.int32)
    matches = slot_index[:, :, None] == positions[None, None, :]
    select = jnp.any(matches, axis=1).astype(jnp.bfloat16)
    combine_w = jnp.sum(
        jnp.where(matches, route_weight[:, :, None].astype(jnp.float32), 0.0), axis=1
    ).astype(jnp.bfloat16)
    expert_rows = lax.dot_general(
        select, activations, (((0,), (0,)), ((), ())), preferred_element_type=jnp.float32
    ).astype(jnp.bfloat16)
    copies = jnp.broadcast_to(
        expert_rows.reshape(send_cap, window, 1, model_width),
        (send_cap, window, SHARDS, model_width),
    )
    copies = copies.reshape(send_cap, window * SHARDS * model_width)
    received = lax.all_to_all(copies, ("node", "ep"), split_axis=1, concat_axis=0, tiled=True)
    gate_act = jnp.dot(received, w_gate, preferred_element_type=jnp.float32)
    up_act = jnp.dot(received, w_up, preferred_element_type=jnp.float32)
    inner_act = (jax.nn.silu(gate_act) * up_act).astype(jnp.bfloat16)
    partial_value = jnp.dot(inner_act, w_down, preferred_element_type=jnp.float32).astype(
        jnp.bfloat16
    )
    returned = lax.all_to_all(
        partial_value, ("node", "ep"), split_axis=0, concat_axis=1, tiled=True
    )
    summed = jnp.sum(
        returned.reshape(send_cap, window, SHARDS, model_width).astype(jnp.float32), axis=2
    )
    expert_out = summed.astype(jnp.bfloat16).reshape(send_cap * window, model_width)
    mixed_out = jnp.dot(combine_w, expert_out, preferred_element_type=jnp.float32)
    return mixed_out.astype(jnp.bfloat16)


def piece_of(width):
    for parts in (4, 2):
        if width % (parts * 128) == 0:
            return width // parts
    return width


def select_rows(node, experts, ids_ref, score_ref, cap_ref):
    ids, scores = ids_ref[...], score_ref[...]
    tokens = ids.shape[1]
    slots = experts * SEND_CAP
    weight = (2.5 * scores / jnp.sum(scores, axis=0, keepdims=True)).astype(jnp.bfloat16)
    weight = weight.astype(jnp.float32)
    line = lax.broadcasted_iota(jnp.int32, (experts * slots, tokens), 0)
    rank_of = line % slots - node * SEND_CAP
    hit = jnp.zeros(line.shape, jnp.float32)
    hit_weight = jnp.zeros(line.shape, jnp.float32)
    limit = jnp.zeros(line.shape, jnp.int32)
    for e in range(experts):
        named = ids == e
        here = line // slots == e
        any_named = jnp.sum(jnp.where(named, 1.0, 0.0), axis=0, keepdims=True)
        its_weight = jnp.sum(jnp.where(named, weight, 0.0), axis=0, keepdims=True)
        hit = jnp.where(here, any_named, hit)
        hit_weight = jnp.where(here, its_weight, hit_weight)
        limit = jnp.where(here, cap_ref[e], limit)
    before = lax.broadcasted_iota(jnp.int32, (tokens, tokens), 0) < lax.broadcasted_iota(
        jnp.int32, (tokens, tokens), 1
    )
    rank = jnp.dot(
        hit.astype(jnp.bfloat16),
        jnp.where(before, 1.0, 0.0).astype(jnp.bfloat16),
        preferred_element_type=jnp.float32,
    ).astype(jnp.int32)
    live = (hit > 0.5) & (rank == rank_of) & (rank_of >= 0) & (rank_of < SEND_CAP) & (rank < limit)
    select = jnp.where(live, 1.0, 0.0).astype(jnp.bfloat16)
    return select, jnp.where(live, hit_weight, 0.0).astype(jnp.bfloat16)


def expert_kernel(
    line, cap_ref, ids_ref, score_ref, act_hbm, wg_hbm, wu_hbm, wd_hbm, out_ref, mix_ref,
    act, wg, wu, wd, gate_sum, up_sum, sent, xb, core_in, part,
    side_in, up_in, down_in, stage, far_up, far_down, far_stage,
    w_sem, core_sem, up_sem, down_sem, side_sem, zrecv_sem, yrecv_sem,
    p_side_sem, p_side_recv, p_up_sem, p_up_recv, p_down_sem, p_down_recv, last_sem, last_recv,
    far_sem, near_sem, near_in, near_stage,
):
    node = lax.axis_index("node")
    ep = lax.axis_index("ep")
    z, y = ep // SIDE, ep % SIDE
    other = 1 - y
    experts, rows, width = sent.shape
    piece = far_stage.shape[2]
    pieces = width // piece
    to_core = {"node": 1 - node}
    to_side = {"ep": z * SIDE + other}
    to_up = {"ep": ep + SIDE}
    to_down = {"ep": ep - SIDE}
    has_up, has_down = z < line - 1, z > 0
    at_end = (z == 0) | (z == line - 1)
    blocks = xb.shape[0] // 2
    half = z // (line // 2)
    near = z + 1 - 2 * (z % 2)
    to_near = {"ep": near * SIDE + y}
    far_end, far_mid = (1 - half) * (line - 1), line // 2 - half

    loads = [
        pltpu.make_async_copy(src, dst, w_sem.at[i])
        for i, (src, dst) in enumerate(((act_hbm, act), (wg_hbm, wg), (wu_hbm, wu), (wd_hbm, wd)))
    ]
    loads[0].start()

    barrier = pltpu.get_barrier_semaphore()
    pl.semaphore_signal(barrier, inc=1, device_id=to_core, device_id_type=MESH)
    pl.semaphore_signal(barrier, inc=1, device_id=to_side, device_id_type=MESH)

    @pl.when(has_up)
    def _():
        pl.semaphore_signal(barrier, inc=1, device_id=to_up, device_id_type=MESH)

    @pl.when(has_down)
    def _():
        pl.semaphore_signal(barrier, inc=1, device_id=to_down, device_id_type=MESH)

    def cols(c):
        return pl.ds(c * piece, piece)

    def remote(src, dst, send, recv, where):
        return pltpu.make_async_remote_copy(
            src_ref=src, dst_ref=dst, send_sem=send, recv_sem=recv,
            device_id=where, device_id_type=MESH,
        )

    def core_copy(c):
        return remote(
            sent.at[1 - node, :, cols(c)], core_in.at[:, cols(c)],
            core_sem.at[0, c], core_sem.at[1, c], to_core,
        )

    def x_copy(o, c, send, recv, where):
        ref = xb.at[o * SIDE + y, :, cols(c)]
        return remote(ref, ref, send.at[o, c], recv.at[o, c], where)

    def x_up(o, c):
        return x_copy(o, c, up_sem, zrecv_sem, to_up)

    def x_down(o, c):
        return x_copy(o, c, down_sem, zrecv_sem, to_down)

    def x_side(o, c):
        return x_copy(o, c, side_sem, yrecv_sem, to_side)

    def far(o, i, where):
        ref = xb.at[o * SIDE + other, :, cols(0)]
        return remote(ref, ref, far_sem.at[i, o], far_sem.at[2, o], where)

    def x_far_up(o):
        return far(o, 0, to_up)

    def x_far_down(o):
        return far(o, 1, to_down)

    select, mix = select_rows(node, experts, ids_ref, score_ref, cap_ref)
    mix_ref[...] = mix
    loads[0].wait()
    for load in loads[1:]:
        load.start()
    for c in range(pieces):
        taken = jnp.dot(select, act[:, cols(c)], preferred_element_type=jnp.float32)
        sent[:, :, cols(c)] = taken.astype(sent.dtype).reshape(experts, rows, piece)
        if c == 0:
            pl.semaphore_wait(barrier, 2 + has_up.astype(jnp.int32) + has_down.astype(jnp.int32))
        core_copy(c).start()
    for c in range(pieces):
        core_copy(c).wait_recv()
        xb[ep, :, cols(c)] = sent[node, :, cols(c)] + core_in[:, cols(c)]
        x_side(z, c).start()
        pl.when(has_up)(lambda: x_up(z, c).start())
        pl.when(has_down)(lambda: x_down(z, c).start())

    x_side(z, 0).wait_recv()
    pl.when(has_up)(lambda: x_far_up(z).start())
    pl.when(has_down)(lambda: x_far_down(z).start())

    def p_side(t, c, own=False):
        src = part.at[t * SIDE + other, :, cols(c)]
        if own:
            src = far_stage.at[t] if c == 0 else near_stage.at[:, cols(c)]
        return remote(
            src, side_in.at[t, :, cols(c)],
            p_side_sem.at[t, c], p_side_recv.at[t, c], to_side,
        )

    def p_up(t, c):
        return remote(
            stage.at[t, :, cols(c)], up_in.at[t, :, cols(c)],
            p_up_sem.at[t, c], p_up_recv.at[t, c], to_up,
        )

    def p_down(t, c):
        return remote(
            stage.at[t, :, cols(c)], down_in.at[t, :, cols(c)],
            p_down_sem.at[t, c], p_down_recv.at[t, c], to_down,
        )

    def p_far_up(t):
        return remote(far_stage.at[t], far_up.at[t], far_sem.at[3, t], far_sem.at[4, t], to_up)

    def p_far_down(t):
        return remote(far_stage.at[t], far_down.at[t], far_sem.at[5, t], far_sem.at[6, t], to_down)

    def p_near(c):
        return remote(
            part.at[near * SIDE + other, :, cols(c)], near_in.at[:, cols(c)],
            near_sem.at[0, c], near_sem.at[1, c], to_near,
        )

    def last(c):
        ref = out_ref.at[node, :, cols(c)]
        return remote(ref, ref, last_sem.at[c], last_recv.at[c], to_core)

    def at_distance(d, act):
        pl.when(z + d < line)(lambda: act(z + d, True))
        pl.when(z - d >= 0)(lambda: act(z - d, False))

    def f32(ref, t, c):
        return ref[t, :, cols(c)].astype(jnp.float32)

    def there(t):
        return f32(part, t * SIDE + other, 0)

    def pass_on(t, c, upward, across):
        across = across and c > 0
        if across:
            p_side(t, c).wait_recv()
        copy, arrived = (p_up, up_in) if upward else (p_down, down_in)
        more, end = (has_down, z == 0) if upward else (has_up, z == line - 1)

        def here():
            own = f32(part, t * SIDE + y, c)
            return own + f32(side_in, t, c) if across else own

        @pl.when(more)
        def _():
            copy(t, c).wait_recv()
            stage[t, :, cols(c)] = (here() + f32(arrived, t, c)).astype(stage.dtype)

        @pl.when(end)
        def _():
            stage[t, :, cols(c)] = here().astype(stage.dtype)

        copy(t, c).start()

    def pass_far(t, upward):
        copy, arrived = (p_far_up, far_up) if upward else (p_far_down, far_down)
        more, end = (has_down, z == 0) if upward else (has_up, z == line - 1)

        @pl.when(more)
        def _():
            copy(t).wait_recv()
            far_stage[t] = (there(t) + arrived[t].astype(jnp.float32)).astype(far_stage.dtype)

        @pl.when(end)
        def _():
            far_stage[t] = there(t).astype(far_stage.dtype)

        copy(t).start()

    def add_gate_up(start, c):
        x = xb[pl.ds(start, blocks), :, cols(c)].reshape(blocks * rows, piece)
        gate_part = jnp.dot(x, wg[cols(c), :], preferred_element_type=jnp.float32)
        up_part = jnp.dot(x, wu[cols(c), :], preferred_element_type=jnp.float32)
        if c == 0:
            gate_sum[...] = gate_part
            up_sum[...] = up_part
        else:
            gate_sum[...] += gate_part
            up_sum[...] += up_part

    def swiglu():
        gate = gate_sum[...]
        return (gate / (1.0 + jnp.exp(-gate)) * up_sum[...]).astype(jnp.bfloat16)

    def put_partial(inner, start, c):
        value = jnp.dot(inner, wd[:, cols(c)], preferred_element_type=jnp.float32)
        part[pl.ds(start, blocks), :, cols(c)] = value.astype(part.dtype).reshape(
            blocks, rows, piece
        )

    def send_near(c):
        if c > 0:
            p_near(c).start()

        @pl.when(z == 0)
        def _():
            pass_on(z + 1, c, True, False)
            if c == 0:
                pass_far(z + 1, True)

        @pl.when(z == line - 1)
        def _():
            pass_on(z - 1, c, False, False)
            if c == 0:
                pass_far(z - 1, False)

    inner = None
    for d in range(1, line):
        if d == line - 1:
            inner = swiglu()
            loads[3].wait()
        for c in range(pieces):
            @pl.when(z - d >= 0)
            def _():
                x_up(z - d, c).wait_recv()
                pl.when(has_up)(lambda: x_up(z - d, c).start())
                if c > 0:
                    x_side(z - d, c).start()

            @pl.when(z + d < line)
            def _():
                x_down(z + d, c).wait_recv()
                pl.when(has_down)(lambda: x_down(z + d, c).start())
                if c > 0:
                    x_side(z + d, c).start()

            if d == line - 2:
                if c == 0:
                    loads[1].wait()
                    loads[2].wait()
                else:
                    x_side(z, c).wait_recv()
                    x_side(near, c).wait_recv()
                add_gate_up(half * blocks, c)
            if d == line - 1:
                put_partial(inner, half * blocks, c)
                pl.when(at_end)(lambda: send_near(c))

        @pl.when(z - d >= 0)
        def _():
            x_far_up(z - d).wait_recv()
            pl.when(has_up)(lambda: x_far_up(z - d).start())

        @pl.when(z + d < line)
        def _():
            x_far_down(z + d).wait_recv()
            pl.when(has_down)(lambda: x_far_down(z + d).start())

    for c in range(pieces):
        if c > 0:
            x_side(far_end, c).wait_recv()
            x_side(far_mid, c).wait_recv()
        add_gate_up((1 - half) * blocks, c)
    inner = swiglu()

    order = list(range(1, pieces)) + [0]
    for c in order:
        put_partial(inner, (1 - half) * blocks, c)
        if c > 0:
            p_side(far_end, c).start()

            @pl.when(jnp.logical_not(at_end))
            def _():
                p_near(c).start()

    for c in range(1, pieces):
        p_side(far_mid, c).start()

    for d in range(line - 1, 1, -1):
        at_distance(d, lambda t, upward: pass_on(t, 0, upward, True))
        at_distance(d, pass_far)
        for c in range(1, pieces):
            at_distance(d, lambda t, upward: pass_on(t, c, upward, True))
        if d == line - 1:
            for c in range(1, pieces):
                p_near(c).wait_recv()
                total = f32(part, z * SIDE + other, c) + near_in[:, cols(c)].astype(jnp.float32)
                near_stage[:, cols(c)] = total.astype(near_stage.dtype)
                p_side(z, c, True).start()

    @pl.when(z == line // 2 - 1)
    def _():
        pass_on(z - 1, 0, False, False)
        pass_far(z - 1, False)
        pass_on(z + 1, 0, True, True)
        pass_far(z + 1, True)
        for c in range(1, pieces):
            pass_on(z - 1, c, False, False)
        for c in range(1, pieces):
            pass_on(z + 1, c, True, True)

    @pl.when(z == line // 2)
    def _():
        pass_on(z + 1, 0, True, False)
        pass_far(z + 1, True)
        pass_on(z - 1, 0, False, True)
        pass_far(z - 1, False)
        for c in range(1, pieces):
            pass_on(z + 1, c, True, False)
        for c in range(1, pieces):
            pass_on(z - 1, c, False, True)

    def far_sum(with_up, with_down):
        total = there(z)
        if with_up:
            total = total + far_up[z].astype(jnp.float32)
        if with_down:
            total = total + far_down[z].astype(jnp.float32)
        far_stage[z] = total.astype(far_stage.dtype)

    def finish(c, with_up, with_down):
        total = f32(part, ep, c) + f32(side_in, z, c)
        if with_up:
            total = total + f32(up_in, z, c)
        if with_down:
            total = total + f32(down_in, z, c)
        out_ref[node, :, cols(c)] = total.astype(out_ref.dtype)

    def by_place(add):
        pl.when(has_down & has_up)(lambda: add(True, True))
        pl.when(z == 0)(lambda: add(False, True))
        pl.when(z == line - 1)(lambda: add(True, False))

    pl.when(has_down)(lambda: p_far_up(z).wait_recv())
    pl.when(has_up)(lambda: p_far_down(z).wait_recv())
    by_place(far_sum)
    p_side(z, 0, True).start()
    for c in order:
        p_side(z, c, True).wait_recv()
        pl.when(has_down)(lambda: p_up(z, c).wait_recv())
        pl.when(has_up)(lambda: p_down(z, c).wait_recv())
        by_place(lambda with_up, with_down: finish(c, with_up, with_down))
        last(c).start()

    def done_far(t, upward):
        pl.when(has_down if upward else has_up)(
            lambda: (x_far_down if upward else x_far_up)(t).wait_send()
        )
        (p_far_up if upward else p_far_down)(t).wait_send()

    def done(t, c, upward):
        pl.when(has_down if upward else has_up)(
            lambda: (x_down if upward else x_up)(t, c).wait_send()
        )
        if c > 0:
            x_side(t, c).wait_send()
        (p_up if upward else p_down)(t, c).wait_send()

    pl.when(has_up)(lambda: x_far_up(z).wait_send())
    pl.when(has_down)(lambda: x_far_down(z).wait_send())
    for d in range(1, line):
        at_distance(d, done_far)
    for c in range(pieces):
        core_copy(c).wait_send()
        x_side(z, c).wait_send()
        pl.when(has_up)(lambda: x_up(z, c).wait_send())
        pl.when(has_down)(lambda: x_down(z, c).wait_send())
        p_side(z, c, True).wait_send()
        if c > 0:
            p_near(c).wait_send()
            p_side(far_end, c).wait_send()
            p_side(far_mid, c).wait_send()
        for d in range(1, line):
            at_distance(d, lambda t, upward: done(t, c, upward))
    for c in order:
        last(c).wait_recv()
        last(c).wait_send()


def run_experts(activations, expert_ids, route_scores, capacity, w_gate, w_up, w_down):
    experts = lax.axis_size("node")
    n_ep = lax.axis_size("ep")
    tokens, width = activations.shape
    rows = experts * SEND_CAP
    line = n_ep // SIDE
    hidden = w_gate.shape[1]
    kind = activations.dtype
    count = n_ep * rows
    piece = piece_of(width)
    pieces = width // piece
    vmem = pltpu.VMEM
    sems = pltpu.SemaphoreType.DMA
    here = pl.BlockSpec(memory_space=pltpu.VMEM)
    return pl.pallas_call(
        functools.partial(expert_kernel, line),
        out_shape=(
            jax.ShapeDtypeStruct((experts, rows, width), kind),
            jax.ShapeDtypeStruct((experts * rows, tokens), jnp.bfloat16),
        ),
        in_specs=[pl.BlockSpec(memory_space=pltpu.SMEM)]
        + [here] * 2
        + [pl.BlockSpec(memory_space=pl.ANY)] * 4,
        out_specs=(here, here),
        scratch_shapes=[
            vmem(activations.shape, kind),
            vmem(w_gate.shape, kind),
            vmem(w_up.shape, kind),
            vmem(w_down.shape, kind),
            vmem((count // 2, hidden), jnp.float32),
            vmem((count // 2, hidden), jnp.float32),
            vmem((experts, rows, width), kind),
            vmem((n_ep, rows, width), kind),
            vmem((rows, width), kind),
            vmem((n_ep, rows, width), kind),
        ]
        + [vmem((line, rows, width), kind)] * 4
        + [vmem((line, rows, piece), kind)] * 3
        + [sems((4,)), sems((2, pieces))]
        + [sems((line, pieces))] * 11
        + [sems((pieces,))] * 2
        + [sems((7, line)), sems((2, pieces)), vmem((rows, width), kind), vmem((rows, width), kind)],
        compiler_params=pltpu.CompilerParams(
            collective_id=0, has_side_effects=True, vmem_limit_bytes=62 * 1024 * 1024 + 400 * 1024
        ),
        cost_estimate=pl.CostEstimate(
            flops=6 * count * width * hidden,
            bytes_accessed=6 * width * hidden,
            transcendentals=count * hidden,
        ),
        name="routed_experts",
    )(capacity, expert_ids.T, route_scores.T, activations, w_gate, w_up, w_down)


def grid_shards(activations, expert_ids, route_scores, capacity, w_gate, w_up, w_down):
    expert_out, combine_w = run_experts(
        activations, expert_ids, route_scores, capacity, w_gate, w_up, w_down
    )
    mixed_out = lax.dot_general(
        combine_w,
        expert_out.reshape(-1, expert_out.shape[2]),
        (((0,), (0,)), ((), ())),
        preferred_element_type=jnp.float32,
    )
    return mixed_out.astype(jnp.bfloat16)


def solution(mesh):
    placed = (
        P(("rep", "node", "ep"), None),
        P(("rep", "node", "ep"), None),
        P(("rep", "node", "ep"), None),
        P(),
        P(None, ("node", "ep")),
        P(None, ("node", "ep")),
        P(("node", "ep"), None),
    )
    fits = mesh.shape["ep"] == SHARDS and mesh.shape["node"] == 2
    return jax.shard_map(
        grid_shards if fits else shards,
        mesh=mesh,
        in_specs=placed,
        out_specs=P(("rep", "node", "ep"), None),
        check_vma=False,
    )
```

```python
import functools

import jax
import jax.numpy as jnp
from jax import lax
from jax.experimental import pallas as pl
from jax.experimental.pallas import tpu as pltpu
from jax.sharding import PartitionSpec as P

MESH = pl.DeviceIdType.MESH
TOPK = 8
SHARDS = 8
SEND_CAP = 8
SIDE = 2


def shards(activations, expert_ids, route_scores, capacity, w_gate, w_up, w_down):
    n_node = lax.axis_size("node")
    n_ep = lax.axis_size("ep")
    window = n_node * (n_ep // SHARDS)
    tok_rows = activations.shape[0]
    model_width = activations.shape[1]
    send_cap = SEND_CAP
    route_weight = (2.5 * route_scores / jnp.sum(route_scores, axis=1, keepdims=True)).astype(
        jnp.bfloat16
    )
    flat_ids = expert_ids.reshape(-1)
    expert_iota = jnp.arange(window, dtype=jnp.int32)
    onehot = (flat_ids[:, None] == expert_iota[None, :]).astype(jnp.int32)
    running = jnp.cumsum(onehot, axis=0)
    ranking = jnp.sum(onehot * running, axis=1) - 1
    limits = jnp.sum(onehot * capacity[:window][None, :], axis=1)
    is_live = (flat_ids < window) & (ranking < limits)
    slot_index = jnp.where(is_live, ranking * window + flat_ids, -1).reshape(tok_rows, TOPK)
    positions = jnp.arange(send_cap * window, dtype=jnp.int32)
    matches = slot_index[:, :, None] == positions[None, None, :]
    select = jnp.any(matches, axis=1).astype(jnp.bfloat16)
    combine_w = jnp.sum(
        jnp.where(matches, route_weight[:, :, None].astype(jnp.float32), 0.0), axis=1
    ).astype(jnp.bfloat16)
    expert_rows = lax.dot_general(
        select, activations, (((0,), (0,)), ((), ())), preferred_element_type=jnp.float32
    ).astype(jnp.bfloat16)
    copies = jnp.broadcast_to(
        expert_rows.reshape(send_cap, window, 1, model_width),
        (send_cap, window, SHARDS, model_width),
    )
    copies = copies.reshape(send_cap, window * SHARDS * model_width)
    received = lax.all_to_all(copies, ("node", "ep"), split_axis=1, concat_axis=0, tiled=True)
    gate_act = jnp.dot(received, w_gate, preferred_element_type=jnp.float32)
    up_act = jnp.dot(received, w_up, preferred_element_type=jnp.float32)
    inner_act = (jax.nn.silu(gate_act) * up_act).astype(jnp.bfloat16)
    partial_value = jnp.dot(inner_act, w_down, preferred_element_type=jnp.float32).astype(
        jnp.bfloat16
    )
    returned = lax.all_to_all(
        partial_value, ("node", "ep"), split_axis=0, concat_axis=1, tiled=True
    )
    summed = jnp.sum(
        returned.reshape(send_cap, window, SHARDS, model_width).astype(jnp.float32), axis=2
    )
    expert_out = summed.astype(jnp.bfloat16).reshape(send_cap * window, model_width)
    mixed_out = jnp.dot(combine_w, expert_out, preferred_element_type=jnp.float32)
    return mixed_out.astype(jnp.bfloat16)


def piece_of(width):
    for size in (1024, 512, 256):
        if width % size == 0:
            return size
    return 128


def select_rows(node, experts, ids_ref, score_ref, cap_ref):
    ids, scores = ids_ref[...], score_ref[...]
    tokens = ids.shape[1]
    slots = experts * SEND_CAP
    weight = (2.5 * scores / jnp.sum(scores, axis=0, keepdims=True)).astype(jnp.bfloat16)
    weight = weight.astype(jnp.float32)
    line = lax.broadcasted_iota(jnp.int32, (experts * slots, tokens), 0)
    rank_of = line % slots - node * SEND_CAP
    hit = jnp.zeros(line.shape, jnp.float32)
    hit_weight = jnp.zeros(line.shape, jnp.float32)
    limit = jnp.zeros(line.shape, jnp.int32)
    for e in range(experts):
        named = ids == e
        here = line // slots == e
        any_named = jnp.sum(jnp.where(named, 1.0, 0.0), axis=0, keepdims=True)
        its_weight = jnp.sum(jnp.where(named, weight, 0.0), axis=0, keepdims=True)
        hit = jnp.where(here, any_named, hit)
        hit_weight = jnp.where(here, its_weight, hit_weight)
        limit = jnp.where(here, cap_ref[e], limit)
    before = lax.broadcasted_iota(jnp.int32, (tokens, tokens), 0) < lax.broadcasted_iota(
        jnp.int32, (tokens, tokens), 1
    )
    rank = jnp.dot(
        hit.astype(jnp.bfloat16),
        jnp.where(before, 1.0, 0.0).astype(jnp.bfloat16),
        preferred_element_type=jnp.float32,
    ).astype(jnp.int32)
    live = (hit > 0.5) & (rank == rank_of) & (rank_of >= 0) & (rank_of < SEND_CAP) & (rank < limit)
    select = jnp.where(live, 1.0, 0.0).astype(jnp.bfloat16)
    return select, jnp.where(live, hit_weight, 0.0).astype(jnp.bfloat16)


def expert_kernel(
    line, cap_ref, ids_ref, score_ref, act_hbm, wg_hbm, wu_hbm, wd_hbm, out_hbm,
    act, wg, wu, wd, gate_sum, up_sum, sent, xb, core_in, part,
    side_in, up_in, down_in, stage, far_up, far_down, far_stage,
    w_sem, core_sem, up_sem, down_sem, side_sem, zrecv_sem, yrecv_sem,
    p_side_sem, p_side_recv, p_up_sem, p_up_recv, p_down_sem, p_down_recv, last_sem, last_recv,
    far_sem, near_sem, near_in, near_stage, out_ref, mixed, out_sem,
):
    node = lax.axis_index("node")
    ep = lax.axis_index("ep")
    z, y = ep // SIDE, ep % SIDE
    other = 1 - y
    experts, rows, width = sent.shape
    piece = far_stage.shape[2]
    pieces = width // piece
    to_core = {"node": 1 - node}
    to_side = {"ep": z * SIDE + other}
    to_up = {"ep": ep + SIDE}
    to_down = {"ep": ep - SIDE}
    has_up, has_down = z < line - 1, z > 0
    at_end = (z == 0) | (z == line - 1)
    blocks = xb.shape[0] // 2
    half = z // (line // 2)
    near = z + 1 - 2 * (z % 2)
    to_near = {"ep": near * SIDE + y}
    far_end, far_mid = (1 - half) * (line - 1), line // 2 - half

    loads = [
        pltpu.make_async_copy(src, dst, w_sem.at[i])
        for i, (src, dst) in enumerate(((act_hbm, act), (wg_hbm, wg), (wu_hbm, wu), (wd_hbm, wd)))
    ]
    loads[0].start()

    barrier = pltpu.get_barrier_semaphore()
    pl.semaphore_signal(barrier, inc=1, device_id=to_core, device_id_type=MESH)
    pl.semaphore_signal(barrier, inc=1, device_id=to_side, device_id_type=MESH)

    @pl.when(has_up)
    def _():
        pl.semaphore_signal(barrier, inc=1, device_id=to_up, device_id_type=MESH)

    @pl.when(has_down)
    def _():
        pl.semaphore_signal(barrier, inc=1, device_id=to_down, device_id_type=MESH)

    def cols(c):
        return pl.ds(c * piece, piece)

    def remote(src, dst, send, recv, where):
        return pltpu.make_async_remote_copy(
            src_ref=src, dst_ref=dst, send_sem=send, recv_sem=recv,
            device_id=where, device_id_type=MESH,
        )

    def core_copy(c):
        return remote(
            sent.at[1 - node, :, cols(c)], core_in.at[:, cols(c)],
            core_sem.at[0, c], core_sem.at[1, c], to_core,
        )

    def x_copy(o, c, send, recv, where):
        ref = xb.at[o * SIDE + y, :, cols(c)]
        return remote(ref, ref, send.at[o, c], recv.at[o, c], where)

    def x_up(o, c):
        return x_copy(o, c, up_sem, zrecv_sem, to_up)

    def x_down(o, c):
        return x_copy(o, c, down_sem, zrecv_sem, to_down)

    def x_side(o, c):
        return x_copy(o, c, side_sem, yrecv_sem, to_side)

    def far(o, i, where):
        ref = xb.at[o * SIDE + other, :, cols(0)]
        return remote(ref, ref, far_sem.at[i, o], far_sem.at[2, o], where)

    def x_far_up(o):
        return far(o, 0, to_up)

    def x_far_down(o):
        return far(o, 1, to_down)

    select, mix = select_rows(node, experts, ids_ref, score_ref, cap_ref)
    loads[0].wait()
    for load in loads[1:]:
        load.start()
    for c in range(pieces):
        taken = jnp.dot(select, act[:, cols(c)], preferred_element_type=jnp.float32)
        sent[:, :, cols(c)] = taken.astype(sent.dtype).reshape(experts, rows, piece)
        if c == 0:
            pl.semaphore_wait(barrier, 2 + has_up.astype(jnp.int32) + has_down.astype(jnp.int32))
        core_copy(c).start()
    for c in range(pieces):
        core_copy(c).wait_recv()
        xb[ep, :, cols(c)] = sent[node, :, cols(c)] + core_in[:, cols(c)]
        x_side(z, c).start()
        pl.when(has_up)(lambda: x_up(z, c).start())
        pl.when(has_down)(lambda: x_down(z, c).start())

    x_side(z, 0).wait_recv()
    pl.when(has_up)(lambda: x_far_up(z).start())
    pl.when(has_down)(lambda: x_far_down(z).start())

    def p_side(t, c, own=False):
        src = part.at[t * SIDE + other, :, cols(c)]
        if own:
            src = far_stage.at[t] if c == 0 else near_stage.at[:, cols(c)]
        return remote(
            src, side_in.at[t, :, cols(c)],
            p_side_sem.at[t, c], p_side_recv.at[t, c], to_side,
        )

    def p_up(t, c):
        return remote(
            stage.at[t, :, cols(c)], up_in.at[t, :, cols(c)],
            p_up_sem.at[t, c], p_up_recv.at[t, c], to_up,
        )

    def p_down(t, c):
        return remote(
            stage.at[t, :, cols(c)], down_in.at[t, :, cols(c)],
            p_down_sem.at[t, c], p_down_recv.at[t, c], to_down,
        )

    def p_far_up(t):
        return remote(far_stage.at[t], far_up.at[t], far_sem.at[3, t], far_sem.at[4, t], to_up)

    def p_far_down(t):
        return remote(far_stage.at[t], far_down.at[t], far_sem.at[5, t], far_sem.at[6, t], to_down)

    def p_near(c):
        return remote(
            part.at[near * SIDE + other, :, cols(c)], near_in.at[:, cols(c)],
            near_sem.at[0, c], near_sem.at[1, c], to_near,
        )

    def last(c):
        ref = out_ref.at[node, :, cols(c)]
        return remote(ref, ref, last_sem.at[c], last_recv.at[c], to_core)

    def at_distance(d, act):
        pl.when(z + d < line)(lambda: act(z + d, True))
        pl.when(z - d >= 0)(lambda: act(z - d, False))

    def f32(ref, t, c):
        return ref[t, :, cols(c)].astype(jnp.float32)

    def there(t):
        return f32(part, t * SIDE + other, 0)

    def pass_on(t, c, upward, across):
        across = across and c > 0
        if across:
            p_side(t, c).wait_recv()
        copy, arrived = (p_up, up_in) if upward else (p_down, down_in)
        more, end = (has_down, z == 0) if upward else (has_up, z == line - 1)

        def here():
            own = f32(part, t * SIDE + y, c)
            return own + f32(side_in, t, c) if across else own

        @pl.when(more)
        def _():
            copy(t, c).wait_recv()
            stage[t, :, cols(c)] = (here() + f32(arrived, t, c)).astype(stage.dtype)

        @pl.when(end)
        def _():
            stage[t, :, cols(c)] = here().astype(stage.dtype)

        copy(t, c).start()

    def pass_far(t, upward):
        copy, arrived = (p_far_up, far_up) if upward else (p_far_down, far_down)
        more, end = (has_down, z == 0) if upward else (has_up, z == line - 1)

        @pl.when(more)
        def _():
            copy(t).wait_recv()
            far_stage[t] = (there(t) + arrived[t].astype(jnp.float32)).astype(far_stage.dtype)

        @pl.when(end)
        def _():
            far_stage[t] = there(t).astype(far_stage.dtype)

        copy(t).start()

    def add_gate_up(start, c):
        x = xb[pl.ds(start, blocks), :, cols(c)].reshape(blocks * rows, piece)
        gate_part = jnp.dot(x, wg[cols(c), :], preferred_element_type=jnp.float32)
        up_part = jnp.dot(x, wu[cols(c), :], preferred_element_type=jnp.float32)
        if c == 0:
            gate_sum[...] = gate_part
            up_sum[...] = up_part
        else:
            gate_sum[...] += gate_part
            up_sum[...] += up_part

    def swiglu():
        gate = gate_sum[...]
        return (gate / (1.0 + jnp.exp(-gate)) * up_sum[...]).astype(jnp.bfloat16)

    def put_partial(inner, start, c):
        value = jnp.dot(inner, wd[:, cols(c)], preferred_element_type=jnp.float32)
        part[pl.ds(start, blocks), :, cols(c)] = value.astype(part.dtype).reshape(
            blocks, rows, piece
        )

    def send_near(c):
        if c > 0:
            p_near(c).start()

        @pl.when(z == 0)
        def _():
            pass_on(z + 1, c, True, False)
            if c == 0:
                pass_far(z + 1, True)

        @pl.when(z == line - 1)
        def _():
            pass_on(z - 1, c, False, False)
            if c == 0:
                pass_far(z - 1, False)

    inner = None
    for d in range(1, line):
        if d == line - 1:
            inner = swiglu()
            loads[3].wait()
        for c in range(pieces):
            @pl.when(z - d >= 0)
            def _():
                x_up(z - d, c).wait_recv()
                pl.when(has_up)(lambda: x_up(z - d, c).start())
                if c > 0:
                    x_side(z - d, c).start()

            @pl.when(z + d < line)
            def _():
                x_down(z + d, c).wait_recv()
                pl.when(has_down)(lambda: x_down(z + d, c).start())
                if c > 0:
                    x_side(z + d, c).start()

            if d == line - 2:
                if c == 0:
                    loads[1].wait()
                    loads[2].wait()
                else:
                    x_side(z, c).wait_recv()
                    x_side(near, c).wait_recv()
                add_gate_up(half * blocks, c)
            if d == line - 1:
                put_partial(inner, half * blocks, c)
                pl.when(at_end)(lambda: send_near(c))

        @pl.when(z - d >= 0)
        def _():
            x_far_up(z - d).wait_recv()
            pl.when(has_up)(lambda: x_far_up(z - d).start())

        @pl.when(z + d < line)
        def _():
            x_far_down(z + d).wait_recv()
            pl.when(has_down)(lambda: x_far_down(z + d).start())

    for c in range(pieces):
        if c > 0:
            x_side(far_end, c).wait_recv()
            x_side(far_mid, c).wait_recv()
        add_gate_up((1 - half) * blocks, c)
    inner = swiglu()

    order = list(range(1, pieces)) + [0]
    for c in order:
        put_partial(inner, (1 - half) * blocks, c)
        if c > 0:
            p_side(far_end, c).start()

            @pl.when(jnp.logical_not(at_end))
            def _():
                p_near(c).start()

    for c in range(1, pieces):
        p_side(far_mid, c).start()

    for d in range(line - 1, 1, -1):
        at_distance(d, lambda t, upward: pass_on(t, 0, upward, True))
        at_distance(d, pass_far)
        for c in range(1, pieces):
            at_distance(d, lambda t, upward: pass_on(t, c, upward, True))
        if d == line - 1:
            for c in range(1, pieces):
                p_near(c).wait_recv()
                total = f32(part, z * SIDE + other, c) + near_in[:, cols(c)].astype(jnp.float32)
                near_stage[:, cols(c)] = total.astype(near_stage.dtype)
                p_side(z, c, True).start()

    @pl.when(z == line // 2 - 1)
    def _():
        pass_on(z - 1, 0, False, False)
        pass_far(z - 1, False)
        pass_on(z + 1, 0, True, True)
        pass_far(z + 1, True)
        for c in range(1, pieces):
            pass_on(z - 1, c, False, False)
        for c in range(1, pieces):
            pass_on(z + 1, c, True, True)

    @pl.when(z == line // 2)
    def _():
        pass_on(z + 1, 0, True, False)
        pass_far(z + 1, True)
        pass_on(z - 1, 0, False, True)
        pass_far(z - 1, False)
        for c in range(1, pieces):
            pass_on(z + 1, c, True, False)
        for c in range(1, pieces):
            pass_on(z - 1, c, False, True)

    def far_sum(with_up, with_down):
        total = there(z)
        if with_up:
            total = total + far_up[z].astype(jnp.float32)
        if with_down:
            total = total + far_down[z].astype(jnp.float32)
        far_stage[z] = total.astype(far_stage.dtype)

    def finish(c, with_up, with_down):
        total = f32(part, ep, c) + f32(side_in, z, c)
        if with_up:
            total = total + f32(up_in, z, c)
        if with_down:
            total = total + f32(down_in, z, c)
        out_ref[node, :, cols(c)] = total.astype(out_ref.dtype)

    def by_place(add):
        pl.when(has_down & has_up)(lambda: add(True, True))
        pl.when(z == 0)(lambda: add(False, True))
        pl.when(z == line - 1)(lambda: add(True, False))

    pl.when(has_down)(lambda: p_far_up(z).wait_recv())
    pl.when(has_up)(lambda: p_far_down(z).wait_recv())
    by_place(far_sum)
    p_side(z, 0, True).start()
    for c in order:
        p_side(z, c, True).wait_recv()
        pl.when(has_down)(lambda: p_up(z, c).wait_recv())
        pl.when(has_up)(lambda: p_down(z, c).wait_recv())
        by_place(lambda with_up, with_down: finish(c, with_up, with_down))
        last(c).start()

    def put_out(c):
        return pltpu.make_async_copy(
            mixed.at[:, cols(c)], out_hbm.at[:, cols(c)], out_sem.at[c]
        )

    for c in order:
        last(c).wait_recv()
        value = lax.dot_general(
            mix, out_ref[:, :, cols(c)].reshape(experts * rows, piece), (((0,), (0,)), ((), ())),
            preferred_element_type=jnp.float32,
        )
        mixed[:, cols(c)] = value.astype(mixed.dtype)
        put_out(c).start()

    def done_far(t, upward):
        pl.when(has_down if upward else has_up)(
            lambda: (x_far_down if upward else x_far_up)(t).wait_send()
        )
        (p_far_up if upward else p_far_down)(t).wait_send()

    def done(t, c, upward):
        pl.when(has_down if upward else has_up)(
            lambda: (x_down if upward else x_up)(t, c).wait_send()
        )
        if c > 0:
            x_side(t, c).wait_send()
        (p_up if upward else p_down)(t, c).wait_send()

    pl.when(has_up)(lambda: x_far_up(z).wait_send())
    pl.when(has_down)(lambda: x_far_down(z).wait_send())
    for d in range(1, line):
        at_distance(d, done_far)
    for c in range(pieces):
        core_copy(c).wait_send()
        x_side(z, c).wait_send()
        pl.when(has_up)(lambda: x_up(z, c).wait_send())
        pl.when(has_down)(lambda: x_down(z, c).wait_send())
        p_side(z, c, True).wait_send()
        if c > 0:
            p_near(c).wait_send()
            p_side(far_end, c).wait_send()
            p_side(far_mid, c).wait_send()
        for d in range(1, line):
            at_distance(d, lambda t, upward: done(t, c, upward))
    for c in order:
        last(c).wait_send()
        put_out(c).wait()


def run_experts(activations, expert_ids, route_scores, capacity, w_gate, w_up, w_down):
    experts = lax.axis_size("node")
    n_ep = lax.axis_size("ep")
    tokens, width = activations.shape
    rows = experts * SEND_CAP
    line = n_ep // SIDE
    hidden = w_gate.shape[1]
    kind = activations.dtype
    count = n_ep * rows
    piece = piece_of(width)
    pieces = width // piece
    vmem = pltpu.VMEM
    sems = pltpu.SemaphoreType.DMA
    here = pl.BlockSpec(memory_space=pltpu.VMEM)
    return pl.pallas_call(
        functools.partial(expert_kernel, line),
        out_shape=jax.ShapeDtypeStruct((tokens, width), kind),
        in_specs=[pl.BlockSpec(memory_space=pltpu.SMEM)]
        + [here] * 2
        + [pl.BlockSpec(memory_space=pl.ANY)] * 4,
        out_specs=pl.BlockSpec(memory_space=pl.ANY),
        scratch_shapes=[
            vmem(activations.shape, kind),
            vmem(w_gate.shape, kind),
            vmem(w_up.shape, kind),
            vmem(w_down.shape, kind),
            vmem((count // 2, hidden), jnp.float32),
            vmem((count // 2, hidden), jnp.float32),
            vmem((experts, rows, width), kind),
            vmem((n_ep, rows, width), kind),
            vmem((rows, width), kind),
            vmem((n_ep, rows, width), kind),
        ]
        + [vmem((line, rows, width), kind)] * 4
        + [vmem((line, rows, piece), kind)] * 3
        + [sems((4,)), sems((2, pieces))]
        + [sems((line, pieces))] * 11
        + [sems((pieces,))] * 2
        + [sems((7, line)), sems((2, pieces)), vmem((rows, width), kind), vmem((rows, width), kind)]
        + [vmem((experts, rows, width), kind), vmem((tokens, width), kind), sems((pieces,))],
        compiler_params=pltpu.CompilerParams(
            collective_id=0, has_side_effects=True, vmem_limit_bytes=62 * 1024 * 1024 + 400 * 1024
        ),
        cost_estimate=pl.CostEstimate(
            flops=6 * count * width * hidden,
            bytes_accessed=6 * width * hidden,
            transcendentals=count * hidden,
        ),
        name="routed_experts",
    )(capacity, expert_ids.T, route_scores.T, activations, w_gate, w_up, w_down)


def grid_shards(activations, expert_ids, route_scores, capacity, w_gate, w_up, w_down):
    return run_experts(
        activations, expert_ids, route_scores, capacity, w_gate, w_up, w_down
    )


def solution(mesh):
    placed = (
        P(("rep", "node", "ep"), None),
        P(("rep", "node", "ep"), None),
        P(("rep", "node", "ep"), None),
        P(),
        P(None, ("node", "ep")),
        P(None, ("node", "ep")),
        P(("node", "ep"), None),
    )
    fits = mesh.shape["ep"] == SHARDS and mesh.shape["node"] == 2
    return jax.shard_map(
        grid_shards if fits else shards,
        mesh=mesh,
        in_specs=placed,
        out_specs=P(("rep", "node", "ep"), None),
        check_vma=False,
    )
```

```python
import functools

import jax
import jax.numpy as jnp
from jax import lax
from jax.experimental import pallas as pl
from jax.experimental.pallas import tpu as pltpu
from jax.sharding import PartitionSpec as P

MESH = pl.DeviceIdType.MESH
TOPK = 8
SHARDS = 8
SEND_CAP = 8
SIDE = 2


def shards(activations, expert_ids, route_scores, capacity, w_gate, w_up, w_down):
    n_node = lax.axis_size("node")
    n_ep = lax.axis_size("ep")
    window = n_node * (n_ep // SHARDS)
    tok_rows = activations.shape[0]
    model_width = activations.shape[1]
    send_cap = SEND_CAP
    route_weight = (2.5 * route_scores / jnp.sum(route_scores, axis=1, keepdims=True)).astype(
        jnp.bfloat16
    )
    flat_ids = expert_ids.reshape(-1)
    expert_iota = jnp.arange(window, dtype=jnp.int32)
    onehot = (flat_ids[:, None] == expert_iota[None, :]).astype(jnp.int32)
    running = jnp.cumsum(onehot, axis=0)
    ranking = jnp.sum(onehot * running, axis=1) - 1
    limits = jnp.sum(onehot * capacity[:window][None, :], axis=1)
    is_live = (flat_ids < window) & (ranking < limits)
    slot_index = jnp.where(is_live, ranking * window + flat_ids, -1).reshape(tok_rows, TOPK)
    positions = jnp.arange(send_cap * window, dtype=jnp.int32)
    matches = slot_index[:, :, None] == positions[None, None, :]
    select = jnp.any(matches, axis=1).astype(jnp.bfloat16)
    combine_w = jnp.sum(
        jnp.where(matches, route_weight[:, :, None].astype(jnp.float32), 0.0), axis=1
    ).astype(jnp.bfloat16)
    expert_rows = lax.dot_general(
        select, activations, (((0,), (0,)), ((), ())), preferred_element_type=jnp.float32
    ).astype(jnp.bfloat16)
    copies = jnp.broadcast_to(
        expert_rows.reshape(send_cap, window, 1, model_width),
        (send_cap, window, SHARDS, model_width),
    )
    copies = copies.reshape(send_cap, window * SHARDS * model_width)
    received = lax.all_to_all(copies, ("node", "ep"), split_axis=1, concat_axis=0, tiled=True)
    gate_act = jnp.dot(received, w_gate, preferred_element_type=jnp.float32)
    up_act = jnp.dot(received, w_up, preferred_element_type=jnp.float32)
    inner_act = (jax.nn.silu(gate_act) * up_act).astype(jnp.bfloat16)
    partial_value = jnp.dot(inner_act, w_down, preferred_element_type=jnp.float32).astype(
        jnp.bfloat16
    )
    returned = lax.all_to_all(
        partial_value, ("node", "ep"), split_axis=0, concat_axis=1, tiled=True
    )
    summed = jnp.sum(
        returned.reshape(send_cap, window, SHARDS, model_width).astype(jnp.float32), axis=2
    )
    expert_out = summed.astype(jnp.bfloat16).reshape(send_cap * window, model_width)
    mixed_out = jnp.dot(combine_w, expert_out, preferred_element_type=jnp.float32)
    return mixed_out.astype(jnp.bfloat16)


def piece_of(width):
    for size in (1024, 512, 256):
        if width % size == 0:
            return size
    return 128


def select_rows(node, experts, ids_ref, score_ref, cap_ref):
    ids, scores = ids_ref[...], score_ref[...]
    tokens = ids.shape[1]
    slots = experts * SEND_CAP
    weight = (2.5 * scores / jnp.sum(scores, axis=0, keepdims=True)).astype(jnp.bfloat16)
    weight = weight.astype(jnp.float32)
    line = lax.broadcasted_iota(jnp.int32, (experts * slots, tokens), 0)
    rank_of = line % slots - node * SEND_CAP
    hit = jnp.zeros(line.shape, jnp.float32)
    hit_weight = jnp.zeros(line.shape, jnp.float32)
    limit = jnp.zeros(line.shape, jnp.int32)
    for e in range(experts):
        named = ids == e
        here = line // slots == e
        any_named = jnp.sum(jnp.where(named, 1.0, 0.0), axis=0, keepdims=True)
        its_weight = jnp.sum(jnp.where(named, weight, 0.0), axis=0, keepdims=True)
        hit = jnp.where(here, any_named, hit)
        hit_weight = jnp.where(here, its_weight, hit_weight)
        limit = jnp.where(here, cap_ref[e], limit)
    before = lax.broadcasted_iota(jnp.int32, (tokens, tokens), 0) < lax.broadcasted_iota(
        jnp.int32, (tokens, tokens), 1
    )
    rank = jnp.dot(
        hit.astype(jnp.bfloat16),
        jnp.where(before, 1.0, 0.0).astype(jnp.bfloat16),
        preferred_element_type=jnp.float32,
    ).astype(jnp.int32)
    live = (hit > 0.5) & (rank == rank_of) & (rank_of >= 0) & (rank_of < SEND_CAP) & (rank < limit)
    select = jnp.where(live, 1.0, 0.0).astype(jnp.bfloat16)
    return select, jnp.where(live, hit_weight, 0.0).astype(jnp.bfloat16)


def expert_kernel(
    line, cap_ref, ids_ref, score_ref, act_hbm, wg_hbm, wu_hbm, wd_hbm, out_ref, mix_ref,
    act, wg, wu, wd, gate_sum, up_sum, sent, xb, core_in, part,
    side_in, up_in, down_in, stage, far_up, far_down, far_stage,
    w_sem, core_sem, up_sem, down_sem, side_sem, zrecv_sem, yrecv_sem,
    p_side_sem, p_side_recv, p_up_sem, p_up_recv, p_down_sem, p_down_recv, last_sem, last_recv,
    far_sem, near_sem, near_in, near_stage,
):
    node = lax.axis_index("node")
    ep = lax.axis_index("ep")
    z, y = ep // SIDE, ep % SIDE
    other = 1 - y
    experts, rows, width = sent.shape
    piece = far_stage.shape[2]
    pieces = width // piece
    to_core = {"node": 1 - node}
    to_side = {"ep": z * SIDE + other}
    to_up = {"ep": ep + SIDE}
    to_down = {"ep": ep - SIDE}
    has_up, has_down = z < line - 1, z > 0
    at_end = (z == 0) | (z == line - 1)
    blocks = xb.shape[0] // 2
    half = z // (line // 2)
    near = z + 1 - 2 * (z % 2)
    to_near = {"ep": near * SIDE + y}
    far_end, far_mid = (1 - half) * (line - 1), line // 2 - half

    loads = [
        pltpu.make_async_copy(src, dst, w_sem.at[i])
        for i, (src, dst) in enumerate(((act_hbm, act), (wg_hbm, wg), (wu_hbm, wu), (wd_hbm, wd)))
    ]
    loads[0].start()

    barrier = pltpu.get_barrier_semaphore()
    pl.semaphore_signal(barrier, inc=1, device_id=to_core, device_id_type=MESH)
    pl.semaphore_signal(barrier, inc=1, device_id=to_side, device_id_type=MESH)

    @pl.when(has_up)
    def _():
        pl.semaphore_signal(barrier, inc=1, device_id=to_up, device_id_type=MESH)

    @pl.when(has_down)
    def _():
        pl.semaphore_signal(barrier, inc=1, device_id=to_down, device_id_type=MESH)

    def cols(c):
        return pl.ds(c * piece, piece)

    def remote(src, dst, send, recv, where):
        return pltpu.make_async_remote_copy(
            src_ref=src, dst_ref=dst, send_sem=send, recv_sem=recv,
            device_id=where, device_id_type=MESH,
        )

    def core_copy(c):
        return remote(
            sent.at[1 - node, :, cols(c)], core_in.at[:, cols(c)],
            core_sem.at[0, c], core_sem.at[1, c], to_core,
        )

    def x_copy(o, c, send, recv, where):
        ref = xb.at[o * SIDE + y, :, cols(c)]
        return remote(ref, ref, send.at[o, c], recv.at[o, c], where)

    def x_up(o, c):
        return x_copy(o, c, up_sem, zrecv_sem, to_up)

    def x_down(o, c):
        return x_copy(o, c, down_sem, zrecv_sem, to_down)

    def x_side(o, c):
        return x_copy(o, c, side_sem, yrecv_sem, to_side)

    def far(o, i, where):
        ref = xb.at[o * SIDE + other, :, cols(0)]
        return remote(ref, ref, far_sem.at[i, o], far_sem.at[2, o], where)

    def x_far_up(o):
        return far(o, 0, to_up)

    def x_far_down(o):
        return far(o, 1, to_down)

    select, mix = select_rows(node, experts, ids_ref, score_ref, cap_ref)
    mix_ref[...] = mix
    loads[0].wait()
    for load in loads[1:]:
        load.start()
    for c in range(pieces):
        taken = jnp.dot(select, act[:, cols(c)], preferred_element_type=jnp.float32)
        sent[:, :, cols(c)] = taken.astype(sent.dtype).reshape(experts, rows, piece)
        if c == 0:
            pl.semaphore_wait(barrier, 2 + has_up.astype(jnp.int32) + has_down.astype(jnp.int32))
        core_copy(c).start()
    for c in range(pieces):
        core_copy(c).wait_recv()
        xb[ep, :, cols(c)] = sent[node, :, cols(c)] + core_in[:, cols(c)]
        pl.when(has_up)(lambda: x_up(z, c).start())
        pl.when(has_down)(lambda: x_down(z, c).start())
        x_side(z, c).start()

    x_side(z, 0).wait_recv()
    pl.when(has_up)(lambda: x_far_up(z).start())
    pl.when(has_down)(lambda: x_far_down(z).start())

    def p_side(t, c, own=False):
        src = part.at[t * SIDE + other, :, cols(c)]
        if own:
            src = far_stage.at[t] if c == 0 else near_stage.at[:, cols(c)]
        return remote(
            src, side_in.at[t, :, cols(c)],
            p_side_sem.at[t, c], p_side_recv.at[t, c], to_side,
        )

    def p_up(t, c):
        return remote(
            stage.at[t, :, cols(c)], up_in.at[t, :, cols(c)],
            p_up_sem.at[t, c], p_up_recv.at[t, c], to_up,
        )

    def p_down(t, c):
        return remote(
            stage.at[t, :, cols(c)], down_in.at[t, :, cols(c)],
            p_down_sem.at[t, c], p_down_recv.at[t, c], to_down,
        )

    def p_far_up(t):
        return remote(far_stage.at[t], far_up.at[t], far_sem.at[3, t], far_sem.at[4, t], to_up)

    def p_far_down(t):
        return remote(far_stage.at[t], far_down.at[t], far_sem.at[5, t], far_sem.at[6, t], to_down)

    def p_near(c):
        return remote(
            part.at[near * SIDE + other, :, cols(c)], near_in.at[:, cols(c)],
            near_sem.at[0, c], near_sem.at[1, c], to_near,
        )

    def last(c):
        ref = out_ref.at[node, :, cols(c)]
        return remote(ref, ref, last_sem.at[c], last_recv.at[c], to_core)

    def at_distance(d, act):
        pl.when(z + d < line)(lambda: act(z + d, True))
        pl.when(z - d >= 0)(lambda: act(z - d, False))

    def f32(ref, t, c):
        return ref[t, :, cols(c)].astype(jnp.float32)

    def there(t):
        return f32(part, t * SIDE + other, 0)

    def pass_on(t, c, upward, across):
        across = across and c > 0
        if across:
            p_side(t, c).wait_recv()
        copy, arrived = (p_up, up_in) if upward else (p_down, down_in)
        more, end = (has_down, z == 0) if upward else (has_up, z == line - 1)

        def here():
            own = f32(part, t * SIDE + y, c)
            return own + f32(side_in, t, c) if across else own

        @pl.when(more)
        def _():
            copy(t, c).wait_recv()
            stage[t, :, cols(c)] = (here() + f32(arrived, t, c)).astype(stage.dtype)

        @pl.when(end)
        def _():
            stage[t, :, cols(c)] = here().astype(stage.dtype)

        copy(t, c).start()

    def pass_far(t, upward):
        copy, arrived = (p_far_up, far_up) if upward else (p_far_down, far_down)
        more, end = (has_down, z == 0) if upward else (has_up, z == line - 1)

        @pl.when(more)
        def _():
            copy(t).wait_recv()
            far_stage[t] = (there(t) + arrived[t].astype(jnp.float32)).astype(far_stage.dtype)

        @pl.when(end)
        def _():
            far_stage[t] = there(t).astype(far_stage.dtype)

        copy(t).start()

    def add_gate_up(start, c):
        x = xb[pl.ds(start, blocks), :, cols(c)].reshape(blocks * rows, piece)
        gate_part = jnp.dot(x, wg[cols(c), :], preferred_element_type=jnp.float32)
        up_part = jnp.dot(x, wu[cols(c), :], preferred_element_type=jnp.float32)
        if c == 0:
            gate_sum[...] = gate_part
            up_sum[...] = up_part
        else:
            gate_sum[...] += gate_part
            up_sum[...] += up_part

    def swiglu():
        gate = gate_sum[...]
        return (gate / (1.0 + jnp.exp(-gate)) * up_sum[...]).astype(jnp.bfloat16)

    def put_partial(inner, start, c):
        value = jnp.dot(inner, wd[:, cols(c)], preferred_element_type=jnp.float32)
        part[pl.ds(start, blocks), :, cols(c)] = value.astype(part.dtype).reshape(
            blocks, rows, piece
        )

    def send_near(c):
        if c > 0:
            p_near(c).start()

        @pl.when(z == 0)
        def _():
            pass_on(z + 1, c, True, False)
            if c == 0:
                pass_far(z + 1, True)

        @pl.when(z == line - 1)
        def _():
            pass_on(z - 1, c, False, False)
            if c == 0:
                pass_far(z - 1, False)

    inner = None
    for d in range(1, line):
        if d == line - 1:
            inner = swiglu()
            loads[3].wait()
        for c in range(pieces):
            @pl.when(z - d >= 0)
            def _():
                x_up(z - d, c).wait_recv()
                pl.when(has_up)(lambda: x_up(z - d, c).start())
                if c > 0:
                    x_side(z - d, c).start()

            @pl.when(z + d < line)
            def _():
                x_down(z + d, c).wait_recv()
                pl.when(has_down)(lambda: x_down(z + d, c).start())
                if c > 0:
                    x_side(z + d, c).start()

            if d == line - 2:
                if c == 0:
                    loads[1].wait()
                    loads[2].wait()
                else:
                    x_side(z, c).wait_recv()
                    x_side(near, c).wait_recv()
                add_gate_up(half * blocks, c)
            if d == line - 1:
                put_partial(inner, half * blocks, c)
                pl.when(at_end)(lambda: send_near(c))

        @pl.when(z - d >= 0)
        def _():
            x_far_up(z - d).wait_recv()
            pl.when(has_up)(lambda: x_far_up(z - d).start())

        @pl.when(z + d < line)
        def _():
            x_far_down(z + d).wait_recv()
            pl.when(has_down)(lambda: x_far_down(z + d).start())

    for c in range(pieces):
        if c > 0:
            x_side(far_end, c).wait_recv()
            x_side(far_mid, c).wait_recv()
        add_gate_up((1 - half) * blocks, c)
    inner = swiglu()

    order = list(range(1, pieces)) + [0]
    for c in order:
        put_partial(inner, (1 - half) * blocks, c)
        if c > 0:
            p_side(far_end, c).start()

            @pl.when(jnp.logical_not(at_end))
            def _():
                p_near(c).start()

    for c in range(1, pieces):
        p_side(far_mid, c).start()

    for d in range(line - 1, 1, -1):
        at_distance(d, lambda t, upward: pass_on(t, 0, upward, True))
        at_distance(d, pass_far)
        for c in range(1, pieces):
            at_distance(d, lambda t, upward: pass_on(t, c, upward, True))
        if d == line - 1:
            for c in range(1, pieces):
                p_near(c).wait_recv()
                total = f32(part, z * SIDE + other, c) + near_in[:, cols(c)].astype(jnp.float32)
                near_stage[:, cols(c)] = total.astype(near_stage.dtype)
                p_side(z, c, True).start()

    @pl.when(z == line // 2 - 1)
    def _():
        pass_on(z - 1, 0, False, False)
        pass_far(z - 1, False)
        pass_on(z + 1, 0, True, True)
        pass_far(z + 1, True)
        for c in range(1, pieces):
            pass_on(z - 1, c, False, False)
        for c in range(1, pieces):
            pass_on(z + 1, c, True, True)

    @pl.when(z == line // 2)
    def _():
        pass_on(z + 1, 0, True, False)
        pass_far(z + 1, True)
        pass_on(z - 1, 0, False, True)
        pass_far(z - 1, False)
        for c in range(1, pieces):
            pass_on(z + 1, c, True, False)
        for c in range(1, pieces):
            pass_on(z - 1, c, False, True)

    def far_sum(with_up, with_down):
        total = there(z)
        if with_up:
            total = total + far_up[z].astype(jnp.float32)
        if with_down:
            total = total + far_down[z].astype(jnp.float32)
        far_stage[z] = total.astype(far_stage.dtype)

    def finish(c, with_up, with_down):
        total = f32(part, ep, c) + f32(side_in, z, c)
        if with_up:
            total = total + f32(up_in, z, c)
        if with_down:
            total = total + f32(down_in, z, c)
        out_ref[node, :, cols(c)] = total.astype(out_ref.dtype)

    def by_place(add):
        pl.when(has_down & has_up)(lambda: add(True, True))
        pl.when(z == 0)(lambda: add(False, True))
        pl.when(z == line - 1)(lambda: add(True, False))

    pl.when(has_down)(lambda: p_far_up(z).wait_recv())
    pl.when(has_up)(lambda: p_far_down(z).wait_recv())
    by_place(far_sum)
    p_side(z, 0, True).start()
    for c in order:
        p_side(z, c, True).wait_recv()
        pl.when(has_down)(lambda: p_up(z, c).wait_recv())
        pl.when(has_up)(lambda: p_down(z, c).wait_recv())
        by_place(lambda with_up, with_down: finish(c, with_up, with_down))
        last(c).start()

    def done_far(t, upward):
        pl.when(has_down if upward else has_up)(
            lambda: (x_far_down if upward else x_far_up)(t).wait_send()
        )
        (p_far_up if upward else p_far_down)(t).wait_send()

    def done(t, c, upward):
        pl.when(has_down if upward else has_up)(
            lambda: (x_down if upward else x_up)(t, c).wait_send()
        )
        if c > 0:
            x_side(t, c).wait_send()
        (p_up if upward else p_down)(t, c).wait_send()

    pl.when(has_up)(lambda: x_far_up(z).wait_send())
    pl.when(has_down)(lambda: x_far_down(z).wait_send())
    for d in range(1, line):
        at_distance(d, done_far)
    for c in range(pieces):
        core_copy(c).wait_send()
        x_side(z, c).wait_send()
        pl.when(has_up)(lambda: x_up(z, c).wait_send())
        pl.when(has_down)(lambda: x_down(z, c).wait_send())
        p_side(z, c, True).wait_send()
        if c > 0:
            p_near(c).wait_send()
            p_side(far_end, c).wait_send()
            p_side(far_mid, c).wait_send()
        for d in range(1, line):
            at_distance(d, lambda t, upward: done(t, c, upward))
    for c in order:
        last(c).wait_recv()
        last(c).wait_send()


def run_experts(activations, expert_ids, route_scores, capacity, w_gate, w_up, w_down):
    experts = lax.axis_size("node")
    n_ep = lax.axis_size("ep")
    tokens, width = activations.shape
    rows = experts * SEND_CAP
    line = n_ep // SIDE
    hidden = w_gate.shape[1]
    kind = activations.dtype
    count = n_ep * rows
    piece = piece_of(width)
    pieces = width // piece
    vmem = pltpu.VMEM
    sems = pltpu.SemaphoreType.DMA
    here = pl.BlockSpec(memory_space=pltpu.VMEM)
    return pl.pallas_call(
        functools.partial(expert_kernel, line),
        out_shape=(
            jax.ShapeDtypeStruct((experts, rows, width), kind),
            jax.ShapeDtypeStruct((experts * rows, tokens), jnp.bfloat16),
        ),
        in_specs=[pl.BlockSpec(memory_space=pltpu.SMEM)]
        + [here] * 2
        + [pl.BlockSpec(memory_space=pl.ANY)] * 4,
        out_specs=(here, here),
        scratch_shapes=[
            vmem(activations.shape, kind),
            vmem(w_gate.shape, kind),
            vmem(w_up.shape, kind),
            vmem(w_down.shape, kind),
            vmem((count // 2, hidden), jnp.float32),
            vmem((count // 2, hidden), jnp.float32),
            vmem((experts, rows, width), kind),
            vmem((n_ep, rows, width), kind),
            vmem((rows, width), kind),
            vmem((n_ep, rows, width), kind),
        ]
        + [vmem((line, rows, width), kind)] * 4
        + [vmem((line, rows, piece), kind)] * 3
        + [sems((4,)), sems((2, pieces))]
        + [sems((line, pieces))] * 11
        + [sems((pieces,))] * 2
        + [sems((7, line)), sems((2, pieces)), vmem((rows, width), kind), vmem((rows, width), kind)],
        compiler_params=pltpu.CompilerParams(
            collective_id=0, has_side_effects=True, vmem_limit_bytes=61 * 1024 * 1024 + 768 * 1024
        ),
        cost_estimate=pl.CostEstimate(
            flops=6 * count * width * hidden,
            bytes_accessed=6 * width * hidden,
            transcendentals=count * hidden,
        ),
        name="routed_experts",
    )(capacity, expert_ids.T, route_scores.T, activations, w_gate, w_up, w_down)


def grid_shards(activations, expert_ids, route_scores, capacity, w_gate, w_up, w_down):
    expert_out, combine_w = run_experts(
        activations, expert_ids, route_scores, capacity, w_gate, w_up, w_down
    )
    mixed_out = lax.dot_general(
        combine_w,
        expert_out.reshape(-1, expert_out.shape[2]),
        (((0,), (0,)), ((), ())),
        preferred_element_type=jnp.float32,
    )
    return mixed_out.astype(jnp.bfloat16)


def solution(mesh):
    placed = (
        P(("rep", "node", "ep"), None),
        P(("rep", "node", "ep"), None),
        P(("rep", "node", "ep"), None),
        P(),
        P(None, ("node", "ep")),
        P(None, ("node", "ep")),
        P(("node", "ep"), None),
    )
    fits = mesh.shape["ep"] == SHARDS and mesh.shape["node"] == 2
    return jax.shard_map(
        grid_shards if fits else shards,
        mesh=mesh,
        in_specs=placed,
        out_specs=P(("rep", "node", "ep"), None),
        check_vma=False,
    )
```
